256 devices in a mesh: dp: 8 (over y, core), tensor: 32 (over x, z).
Axes of the slice: x: 4, y: 4, z: 8, core: 2. Of those that a mesh axis runs over, the one named last changes fastest.
Arguments:
- hidden: bfloat16 [8192, 2048], P(('dp', 'tensor')), parts along dimension 0, may hold values from -6 to 6
- norm_gain: bfloat16 [2048], replicated, may hold values from 0.099609375 to 1.8984375
- router_weight: bfloat16 [2048, 8], replicated, may hold values from -0.125 to 0.125
- kv_weight: bfloat16 [2048, 4096], P(None, 'tensor'), may hold values from -0.125 to 0.125
- query_weight: bfloat16 [2048, 16384], P(None, 'tensor'), may hold values from -0.125 to 0.125
- out_weight: bfloat16 [16384, 2048], P('tensor'), may hold values from -0.5 to 0.5
- routes: int32 [8192, 2], P('dp'), parts along dimension 0, may hold values from 0 to 7, all different within a row; in each aligned block of 1024 rows (0 to 1023, 1024 to 2047, ...) at most 384 rows name the same one
- segment_ids: int32 [8192], P('dp'), parts along dimension 0, may hold values from 0 to 3, never falling along the last dimension, each value on 1 to 512 neighbouring positions
- page_table: int32 [64], P('dp'), parts along dimension 0, may hold values from 0 to 15, as said below
- kv_cache: bfloat16 [128, 128, 4096], P('dp', None, 'tensor'), parts along dimension 0, may hold values from -6 to 6
Outputs:
- attended_out: bfloat16 [8192, 2048], P(('dp', 'tensor')), parts along dimension 0
- new_cache: bfloat16 [128, 128, 4096], P('dp', None, 'tensor'), parts along dimension 0
The draws below stay inside these ranges and needn't reach their ends.
There are 8 independent parts, one for each index of `dp`. The reference program is written for one: setup_inputs(seed, part) draws one part's arguments, and reference() takes and returns one part's arrays. A program takes and returns all parts, laid end to end along the dimension named above; an argument that names none is the same for every part. Nothing has to cross between parts.
Inputs may be any that keep to these rules, and one draw needn't show every extreme that they name: `routes`: no expert is named by more than 384 tokens of a batch, and one is named by exactly 384; a token names two different experts. `segment_ids`: ids never fall along the pack; each prompt has 1 to 512 tokens and one has exactly 512. `page_table`: distinct pages.
All inputs are finite; a program needn't handle non-finite values.
Results may differ from the reference program's by a relative error of at most 0.025.
Values may be sent and summed in bfloat16 or wider, within the bound.
A program may use at most 128 MiB of HBM per device.

```python
import math
import jax
import jax.numpy as jnp
import numpy as np
from jax import lax

D = 2048
HD = 128
KVH = 16
EA = 8
TOPK = 2
PAGE = 128
S = 1024
CAP = 384
BLOCKS = 8
NPAGES = 16
SEGS = 4
SEG_MOST = 512
N_TENSOR = 32


def draw_page_table(key, part):
    return jax.random.permutation(key, NPAGES)[:BLOCKS].astype(jnp.int32)


def block_scale(key, extent, pieces, smallest, top_value):
    level = 1.0
    for axis_at, blocks in pieces:
        draws = jax.random.uniform(jax.random.fold_in(jax.random.fold_in(key, 6), axis_at), (blocks,), jnp.float32, smallest / len(pieces), top_value / len(pieces))
        level = level * jnp.repeat(jnp.exp(draws), extent[axis_at] // blocks).reshape((-1,) + (1,) * (len(extent) - 1 - axis_at))
    return level


def split_up(amount, total, limit, lean):
    loads = [(1 << 20) // math.isqrt(rank ** lean) + 1 for rank in range(2, amount + 1)]
    spare, counts = total - limit - (amount - 1), [1] * (amount - 1)
    while spare > 0:
        free = [i for i in range(amount - 1) if counts[i] < limit]
        whole, left = sum([loads[i] for i in free]), spare
        for i in free:
            addition = min(limit - counts[i], max(1, left * loads[i] // whole), spare)
            counts[i] = counts[i] + addition
            spare = spare - addition
    return np.array([limit] + counts)


def uneven_parts(stream_key, amount, total, limit, slope):
    if amount == 2:
        one = jax.random.randint(stream_key, (), max(1, total - limit), min(limit, total - 1) + 1)
        return jnp.stack([one, total - one])
    lengths = jnp.asarray(split_up(amount, total, limit, slope), jnp.int32)
    couples = (amount - 1) // 2
    giver, receiver = lengths[1:1 + 2 * couples:2], lengths[2:2 + 2 * couples:2]
    room = jnp.minimum(giver - 1, limit - receiver)
    moved = jax.random.randint(jax.random.fold_in(stream_key, 1), (couples,), 0, 1 << 20) % (room + 1)
    lengths = lengths.at[1:1 + 2 * couples:2].set(giver - moved).at[2:2 + 2 * couples:2].set(receiver + moved)
    return lengths[jax.random.permutation(jax.random.fold_in(stream_key, 2), amount)]


def assign_block(own_key, own, number, rows, amount, top, reach, slope):
    sequence = jax.random.permutation(own_key, amount)
    heavy_load, usual = shares(amount, rows * top, reach, slope, True), shares(amount, rows * top, reach, slope, False)
    places = jnp.arange(amount)

    def named(sizes, rotation):
        used = int((sizes > 0).sum())
        fixed = max(1, used // 4)
        shifted = fixed + (places - fixed + rotation * (used - fixed)) % max(1, amount - fixed)
        return jnp.zeros((amount,), jnp.int32).at[sequence[jnp.where(places < fixed, places, shifted)]].set(jnp.asarray(sizes, jnp.int32))

    sizes = jnp.where(number % 4 == 0, named(heavy_load, number // 4), named(usual, number - number // 4 - 1))
    mixed = jax.random.permutation(jax.random.fold_in(own, 3), amount)
    donor, sink = mixed[0:amount // 2 * 2:2], mixed[1:amount // 2 * 2:2]
    room = jnp.minimum(sizes[donor] - 1, reach - sizes[sink]) // 2
    room = jnp.where((donor == sequence[0]) | (sink == sequence[0]) | (sizes[sink] == 0), 0, jnp.maximum(room, 0))
    shifted = jax.random.randint(jax.random.fold_in(own, 4), (amount // 2,), 0, 1 << 20) % (room + 1)
    sizes = sizes.at[donor].add(-shifted).at[sink].add(shifted)
    items = jnp.searchsorted(jnp.cumsum(sizes), jnp.arange(rows * top), side="right").astype(jnp.int32)
    listing = items.reshape(top, rows).T
    listing = listing[jax.random.permutation(jax.random.fold_in(own, 1), rows)]
    rotation = jax.random.randint(jax.random.fold_in(own, 2), (rows, 1), 0, top)
    return jnp.take_along_axis(listing, (jnp.arange(top)[None, :] + rotation) % top, axis=1)


def shares(number_of, total, most, skew, full):
    weights = [(1 << 20) // math.isqrt(rank ** skew) + 1 for rank in range(1, number_of + 1)]
    largest = most if full else min(most, max(-(-total // number_of), total * weights[0] // sum(weights)))
    least = 1 if total - largest >= number_of - 1 else 0
    counts, rest = [largest] + [least] * (number_of - 1), total - largest - least * (number_of - 1)
    while rest > 0:
        movable = [i for i in range(1, number_of) if counts[i] < largest] or [i for i in range(1, number_of) if counts[i] < most]
        whole, budget = sum([weights[i] for i in movable]), rest
        for i in movable:
            extra = min(most - counts[i], max(1, budget * weights[i] // whole), rest)
            counts[i] = counts[i] + extra
            rest = rest - extra
    return np.array(counts)


def noise(stream_key, shape, deviation, limit, cuts=(), kind=jnp.bfloat16):
    drawn = deviation * jax.random.normal(stream_key, shape, jnp.float32)
    if cuts:
        drawn = drawn * block_scale(stream_key, shape, cuts, -0.22, 0.18)
    return jnp.clip(drawn, -limit, limit).astype(kind)


def setup_inputs(seed: int = 0, part: int = 0) -> dict:
    keys = jax.random.split(jax.random.key(seed), 11)
    part_keys = jax.random.split(jax.random.fold_in(keys[10], part), 11)
    hidden = noise(part_keys[0], (S, D), 1.0, 6.0, ((0, 32),))
    norm_gain = jnp.clip(1.0 + 0.18 * jax.random.normal(keys[1], (D,), jnp.float32), 0.099609375, 1.8984375).astype(jnp.bfloat16)
    router_weight = noise(keys[2], (D, EA), D ** -0.5, 0.125)
    kv_weight = noise(keys[3], (D, 2 * KVH * HD), D ** -0.5, 0.125, ((1, 32),))
    query_weight = noise(keys[4], (D, KVH * EA * HD), D ** -0.5, 0.125, ((1, 32),))
    out_weight = noise(keys[5], (KVH * EA * HD, D), HD ** -0.5, 0.5, ((0, 32),))
    routes_keys = jax.random.split(jax.random.fold_in(part_keys[6], 1), S // S)
    routes_turns = jax.random.permutation(jax.random.fold_in(part_keys[6], 3), S // S)
    routes = jax.vmap(lambda own, number: assign_block(jax.random.fold_in(part_keys[6], 2), own, number, S, EA, TOPK, CAP, 2))(routes_keys, routes_turns).reshape((S, TOPK))
    segment_ids = jnp.searchsorted(jnp.cumsum(uneven_parts(part_keys[7], SEGS, S, SEG_MOST, 2)), jnp.arange(S), side="right").astype(jnp.int32)
    page_table = draw_page_table(jax.random.fold_in(jax.random.fold_in(keys[10], part), 71), part)
    kv_cache = noise(part_keys[9], (NPAGES, PAGE, 2 * KVH * HD), 1.0, 6.0, ((2, 32),))
    return {"hidden": hidden, "norm_gain": norm_gain, "router_weight": router_weight, "kv_weight": kv_weight, "query_weight": query_weight, "out_weight": out_weight, "routes": routes, "segment_ids": segment_ids, "page_table": page_table, "kv_cache": kv_cache}


def normalize(hidden, norm_gain):
    values = hidden.astype(jnp.float32)
    factor = lax.rsqrt(lax.optimization_barrier(jnp.mean(values * values, axis=-1, keepdims=True)) + 1e-05)
    return (values * factor * norm_gain.astype(jnp.float32)).astype(jnp.bfloat16)

def gate_table(normed, router_weight, routes):
    logits = jnp.dot(normed, router_weight, preferred_element_type=jnp.float32)
    chosen = jnp.take_along_axis(logits, routes, axis=1)
    weights = jax.nn.softmax(chosen, axis=-1)
    expert_ids = jnp.arange(router_weight.shape[1], dtype=jnp.int32)
    onehot = (routes[:, :, None] == expert_ids[None, None, :]).astype(jnp.float32)
    return lax.optimization_barrier(jnp.sum(weights[:, :, None] * onehot, axis=1))

def positions_of(segment_ids):
    index_row = jnp.arange(segment_ids.shape[0], dtype=jnp.int32)
    starts_here = jnp.concatenate([jnp.ones((1,), dtype=bool), segment_ids[1:] != segment_ids[:-1]])
    segment_start = lax.cummax(jnp.where(starts_here, index_row, 0), axis=0)
    return index_row - segment_start

def rotate(values, positions):
    half_width = values.shape[-1] // 2
    frequency = 10000.0 ** (-jnp.arange(half_width, dtype=jnp.float32) / half_width)
    angles = positions.astype(jnp.float32)[:, None] * frequency[None, :]
    angles = angles.reshape((values.shape[0],) + (1,) * (values.ndim - 2) + (half_width,))
    cosine = jnp.cos(angles)
    sine_part = jnp.sin(angles)
    leading = values[..., :half_width]
    trailing = values[..., half_width:]
    return jnp.concatenate([leading * cosine - trailing * sine_part, trailing * cosine + leading * sine_part], axis=-1)

def expert_slots(routes, expert, capacity):
    is_hit = jnp.any(routes == expert, axis=1)
    running = jnp.cumsum(is_hit.astype(jnp.int32))
    placed = jnp.where(is_hit, running - 1, capacity)
    index_row = jnp.arange(routes.shape[0], dtype=jnp.int32)
    slot_tok = jnp.zeros((capacity + 1,), jnp.int32).at[placed].set(index_row)[:capacity]
    is_valid = jnp.arange(capacity, dtype=jnp.int32) < running[-1]
    return (slot_tok, is_valid)

def attend(queries, key_rows, value_rows, allowed):
    scores = jnp.dot(queries, key_rows.T, preferred_element_type=jnp.float32)
    scores = jnp.where(allowed, scores, -1e+30)
    probabilities = jax.nn.softmax(scores, axis=-1).astype(jnp.bfloat16)
    return jnp.dot(probabilities, value_rows, preferred_element_type=jnp.float32)

def reference(hidden, norm_gain, router_weight, kv_weight, query_weight, out_weight, routes, segment_ids, page_table, kv_cache):
    normed = normalize(hidden, norm_gain)
    gates = gate_table(normed, router_weight, routes)
    positions = positions_of(segment_ids)
    kv_full = jnp.dot(normed, kv_weight, preferred_element_type=jnp.float32).reshape(S, KVH, 2, HD)
    kv_rows = jnp.stack([rotate(kv_full[:, :, 0], positions), kv_full[:, :, 1]], axis=2).astype(jnp.bfloat16)
    new_cache = kv_cache.at[page_table].set(kv_rows.reshape(BLOCKS, PAGE, KVH * 2 * HD))
    key_all = kv_rows[:, :, 0]
    value_all = kv_rows[:, :, 1]
    index_row = jnp.arange(S, dtype=jnp.int32)
    per_group = KVH * EA // N_TENSOR
    scale_factor = HD ** (-0.5)

    def pair_term(partial_value, pair):
        head_index = pair // EA
        expert = pair % EA
        slot_tok, is_valid = expert_slots(routes, expert, CAP)
        queries = jnp.dot(normed[slot_tok], lax.dynamic_slice_in_dim(query_weight, pair * HD, HD, 1), preferred_element_type=jnp.float32)
        queries = (rotate(queries, positions[slot_tok]) * scale_factor).astype(jnp.bfloat16)
        keys_here = lax.dynamic_index_in_dim(key_all, head_index, 1, keepdims=False)
        values_here = lax.dynamic_index_in_dim(value_all, head_index, 1, keepdims=False)
        allowed = (segment_ids[slot_tok][:, None] == segment_ids[None, :]) & (index_row[None, :] <= slot_tok[:, None])
        attended = attend(queries, keys_here, values_here, allowed)
        gate_here = gates[slot_tok, expert] * is_valid.astype(jnp.float32)
        gated = (attended * gate_here[:, None]).astype(jnp.bfloat16)
        term_rows = jnp.dot(gated, lax.dynamic_slice_in_dim(out_weight, pair * HD, HD, 0), preferred_element_type=jnp.float32)
        target = jnp.where(is_valid, slot_tok, S)
        return (partial_value.at[target].add(term_rows, mode='drop'), None)

    def group_term(total, group):
        pairs_here = group * per_group + jnp.arange(per_group, dtype=jnp.int32)
        partial_value, _ = lax.scan(pair_term, jnp.zeros((S, D), jnp.float32), pairs_here)
        rounded = lax.optimization_barrier(partial_value.astype(jnp.bfloat16))
        return (total + rounded.astype(jnp.float32), None)
    total, _ = lax.scan(group_term, jnp.zeros((S, D), jnp.float32), jnp.arange(N_TENSOR, dtype=jnp.int32))
    attended_out = (hidden.astype(jnp.float32) + total).astype(jnp.bfloat16)
    return (attended_out, new_cache)
```

```python
import functools

import jax
import jax.numpy as jnp
import numpy as np
from jax import lax
from jax.experimental import pallas as pl
from jax.experimental.pallas import tpu as pltpu
from jax.sharding import PartitionSpec as P

NX, NZ, ROWS, D, HD = 4, 8, 32, 2048, 128
EXPERTS = 4
HALF = ROWS // 2
X_OFFSETS = (0, -1, 1, -2)
Z_OFFSETS = (0, -1, 1, -2, 2, -3, 3, -4)
SEND_US, LATENCY_US = 1.31, 1.0


def gather_tasks():
    tasks = []
    for half in "AB":
        for i in X_OFFSETS:
            for j in Z_OFFSETS:
                sends = []
                if half == "A":
                    if j == 0 and i in (0, -1):
                        sends.append(("x+", (half, i - 1, 0)))
                    if j == 0 and i == 0:
                        sends.append(("x-", (half, 1, 0)))
                if -4 < j <= 0 and (half == "A" or i == 0):
                    sends.append(("z+", (half, i, j - 1)))
                if 0 <= j < 3 and (half == "A" or i == 0):
                    sends.append(("z-", (half, i, j + 1)))
                if half == "B":
                    if i in (0, -1):
                        sends.append(("x+", (half, i - 1, j)))
                    if i == 0:
                        sends.append(("x-", (half, 1, j)))
                own = i == 0 and j == 0
                tasks.append(
                    dict(
                        name=("recv", half, i, j),
                        deps=[] if own else [(half, i, j)],
                        after=[("norm",)] if own else [],
                        sends=sends,
                        block=(half, i, j),
                        cost=0.05,
                    )
                )
    return tasks


def reduce_tasks():
    tasks = []

    def add(half, i, j, deps, sends, cost):
        tasks.append(
            dict(name=("sum", half, i, j, len(tasks)), deps=deps, after=[("attend", i)], sends=sends, block=(half, i, j), cost=cost)
        )

    for i in (2, -1, 1, 0):
        for k in (4, 3, 2, 1):
            add("A", i, k, [("A", "L", i, k)] if k < 4 else [], [("z+", ("A", "L", i, k - 1))], 0.1)
        for k in (-3, -2, -1):
            add("A", i, k, [("A", "S", i, k)] if k > -3 else [], [("z-", ("A", "S", i, k + 1))], 0.1)
        deps = [("A", "L", i, 0), ("A", "S", i, 0)]
        if i == 1:
            deps.append(("A", "X", 1))
        if i == 0:
            deps += [("A", "X", 0), ("A", "Y", 0)]
        sends = {2: [("x+", ("A", "X", 1))], -1: [("x-", ("A", "Y", 0))], 1: [("x+", ("A", "X", 0))], 0: []}[i]
        add("A", i, 0, deps, sends, 0.15)
    for j in (4, -3, 3, -2, 2, -1, 1, 0):
        add("B", 2, j, [], [("x+", ("B", "L", 1, j))], 0.1)
        add("B", -1, j, [], [("x-", ("B", "S", 0, j))], 0.1)
        add("B", 1, j, [("B", "L", 1, j)], [("x+", ("B", "L", 0, j))], 0.1)
        deps = [("B", "L", 0, j), ("B", "S", 0, j)]
        sends = []
        if j > 0:
            deps += [("B", "Z", j)] if j < 4 else []
            sends = [("z+", ("B", "Z", j - 1))]
        elif j < 0:
            deps += [("B", "W", j)] if j > -3 else []
            sends = [("z-", ("B", "W", j + 1))]
        else:
            deps += [("B", "Z", 0), ("B", "W", 0)]
        add("B", 0, j, deps, sends, 0.15)
    return tasks


def compute_tasks():
    tasks = [dict(name=("norm",), after=[], cost=1.0)]
    tasks += [dict(name=("setup", n), after=[], cost=1.0) for n in range(4)]
    for j in Z_OFFSETS:
        after = [("recv", half, i, j) for half in "AB" for i in X_OFFSETS] + [("setup", n) for n in range(4)]
        tasks.append(dict(name=("project", j), after=after, cost=0.9))
    everything = [("project", j) for j in Z_OFFSETS]
    tasks.append(dict(name=("swap",), after=everything, cost=1.5))
    for i in (2, -1, 1, 0):
        tasks.append(dict(name=("attend", i), after=[("swap",)], cost=2.0))
    tasks.append(dict(name=("cache",), after=[("swap",), ("attend", 0)], cost=1.0))
    return tasks


@functools.cache
def plan():
    moves, work = gather_tasks() + reduce_tasks(), compute_tasks()
    clock, done, arrived, free, order = 0.0, set(), {}, {}, []
    while moves or work:
        best = None
        for task in moves:
            if all(a in done for a in task["after"]) and all(d in arrived for d in task["deps"]):
                at = max([arrived[d] for d in task["deps"]], default=0.0)
                if best is None or at < best[0]:
                    best = (at, task)
        ready = best is not None and best[0] <= clock
        task = None
        if not ready:
            task = next((w for w in work if all(a in done for a in w["after"])), None)
        if task is None:
            clock, task = max(clock, best[0]), best[1]
            moves.remove(task)
        else:
            work.remove(task)
        clock += task["cost"]
        for link, key in task.get("sends", []):
            begin = max(clock, free.get(link, 0.0))
            free[link] = begin + SEND_US
            arrived[key] = begin + SEND_US + LATENCY_US
        done.add(task["name"])
        order.append(task)
    return order, clock


GATHER_KEYS = [t["block"] for t in gather_tasks() if t["deps"]]
REDUCE_KEYS = [key for t in reduce_tasks() for _, key in t["sends"]]


def layer(
    hidden, gain, router, kv_weight, query_weight, out_weight, routes, segments, frequency, pages, cache,
    out, new_cache,
    full, part, landed, weight, out_w, pool, kv, query, cosine, sine, route, gate, mixed,
    gather_send, gather_recv, reduce_send, reduce_recv, kv_send, kv_recv, load, store,
):
    me = lax.axis_index("tensor")
    turn = 1 - 2 * lax.rem(lax.axis_index("dp"), 2)
    x, z = me // NZ, lax.rem(me, NZ)
    parity = lax.rem(z, 2)
    base = parity * EXPERTS

    def fx(i):
        return lax.rem(x + turn * i + NX, NX)

    def fz(j):
        return lax.rem(z + turn * j + NZ, NZ)

    links = {
        "x+": fx(1) * NZ + z,
        "x-": fx(-1) * NZ + z,
        "z+": x * NZ + fz(1),
        "z-": x * NZ + fz(-1),
    }
    partner = x * NZ + z + 1 - 2 * parity

    barrier = pltpu.get_barrier_semaphore()
    for device in links.values():
        pl.semaphore_signal(barrier, inc=1, device_id={"tensor": device}, device_id_type=pl.DeviceIdType.MESH)

    loads = [
        pltpu.make_async_copy(query_weight, weight.at[:, 0:512], load.at[0]),
        pltpu.make_async_copy(kv_weight, weight.at[:, 512:640], load.at[1]),
        pltpu.make_async_copy(out_weight, out_w, load.at[2]),
        pltpu.make_async_copy(cache, pool, load.at[3]),
    ]
    for copy in loads:
        copy.start()

    def rows_of(half):
        return pl.ds(0 if half == "A" else HALF, HALF)

    def remote(src, dst, send, recv, device):
        return pltpu.make_async_remote_copy(
            src_ref=src, dst_ref=dst, send_sem=send, recv_sem=recv,
            device_id={"tensor": device}, device_id_type=pl.DeviceIdType.MESH,
        )

    lane = lax.broadcasted_iota(jnp.int32, (128, 128), 1)
    sub = lax.broadcasted_iota(jnp.int32, (128, 128), 0)
    low = lane < HD // 2
    waiting = []

    def norm():
        values = hidden[...].astype(jnp.float32)
        factor = lax.rsqrt(jnp.mean(values * values, axis=-1, keepdims=True) + 1e-05)
        full[z, x] = (values * factor * gain[...].astype(jnp.float32)).astype(jnp.bfloat16)
        pl.semaphore_wait(barrier, 4)

    def setup(n):
        seg = segments[...]
        starts = [jnp.sum((seg < s).astype(jnp.float32), axis=1, keepdims=True) for s in (1, 2, 3)]
        for b in (2 * n, 2 * n + 1):
            token = (sub + b * 128).astype(jnp.float32)
            start = jnp.zeros_like(token)
            for s in starts:
                start = jnp.maximum(start, jnp.where(token >= s, s, 0.0))
            first = routes[0:1, b * 128 : b * 128 + 128].astype(jnp.float32)
            second = routes[1:2, b * 128 : b * 128 + 128].astype(jnp.float32)
            columns = jnp.where(sub == 0, first, jnp.where(sub == 1, second, 0.0)).T
            at = (b // 2, pl.ds(b % 2 * 4, 4))
            route[at] = jnp.where(lane == 2, start, columns).reshape(4, 32, 128)
            angle = (token - start) * frequency[...]
            k = jnp.floor(angle * 0.6366197723675814 + 0.5)
            r = angle - k * 1.5703125
            r = r - k * 4.837512969970703e-4
            r = r - k * 7.549789954891882e-8
            w = r * r
            sin = r + r * w * (-1.6666654611e-1 + w * (8.3321608736e-3 - w * 1.9515295891e-4))
            cos = 1.0 - 0.5 * w + w * w * (4.166664568298827e-2 + w * (-1.388731625493765e-3 + w * 2.443315711809948e-5))
            quarter = k - 4.0 * jnp.floor(k * 0.25)
            odd = (quarter == 1.0) | (quarter == 3.0)
            c = jnp.where(odd, sin, cos)
            s = jnp.where(odd, cos, sin)
            c = jnp.where((quarter == 1.0) | (quarter == 2.0), -c, c)
            s = jnp.where(quarter >= 2.0, -s, s)
            cosine[at] = c.reshape(4, 32, 128)
            sine[at] = jnp.where(low, -s, s).reshape(4, 32, 128)
        for c in range(4 * n, 4 * n + 4):
            block = router[:, c * 128 : c * 128 + 128].astype(jnp.float32)
            block = jnp.concatenate([block, jnp.zeros((120, 128), jnp.float32)], axis=0)
            weight[c * 128 : c * 128 + 128, 640:768] = block.T.astype(jnp.bfloat16)
        if n == 0:
            kv[:, 0:2] = jnp.zeros((2, 2, NZ, ROWS, HD), jnp.bfloat16)
        if n == 3:
            for copy in loads:
                copy.wait()

    def rotate(values, c, s):
        return values * c + pltpu.roll(values, HD // 2, 1) * s

    def project(j):
        za = fz(j)
        at = (slice(None), pl.ds(za, 1))
        made = jnp.dot(full[za].reshape(128, D), weight[...], preferred_element_type=jnp.float32)
        picks = route[at].reshape(128, 128)
        c, s = cosine[at].reshape(128, 128), sine[at].reshape(128, 128)
        for n in range(2):
            local = picks[:, n : n + 1] - base.astype(jnp.float32)
            values = jnp.zeros((128, HD), jnp.float32)
            for e in range(EXPERTS):
                values = jnp.where(local == float(e), made[:, e * HD : e * HD + HD], values)
            values = rotate(values, c, s) * (HD**-0.5)
            query[(n, *at)] = values.astype(jnp.bfloat16).reshape(4, 1, 32, 128)
        own = made[:, 512:640]
        own = jnp.where(parity == 0, rotate(own, c, s), own)
        kv[parity, 2:6, pl.ds(za, 1)] = own.astype(jnp.bfloat16).reshape(4, 1, 32, 128)
        logits = made[:, 640:768]
        lanes = lane.astype(jnp.float32)
        first = jnp.sum(jnp.where(lanes == picks[:, 0:1], logits, 0.0), axis=1, keepdims=True)
        second = jnp.sum(jnp.where(lanes == picks[:, 1:2], logits, 0.0), axis=1, keepdims=True)
        top = jnp.maximum(first, second)
        first, second = jnp.exp(first - top), jnp.exp(second - top)
        total = first + second
        gate[at] = jnp.where(lane == 0, first / total, second / total).reshape(4, 1, 32, 128)
        place = kv.at[parity, 2:6, za]
        copy = remote(place, place, kv_send.at[j % NZ], kv_recv.at[j % NZ], partner)
        copy.start()
        waiting.append(copy)

    def swap():
        for j in Z_OFFSETS:
            zp = lax.rem(z + 1 - 2 * parity + turn * j + NZ, NZ)
            place = kv.at[1 - parity, 2:6, zp]
            remote(place, place, kv_send.at[j % NZ], kv_recv.at[j % NZ], partner).wait_recv()

    def attend(i):
        xa = fx(i)
        for half in range(2):
            at = (xa, pl.ds(half * 4, 4))
            keys = kv[0, pl.ds(xa, 3)].reshape(768, HD)[half * 128 : half * 128 + 640]
            values = kv[1, pl.ds(xa, 3)].reshape(768, HD)[half * 128 : half * 128 + 640]
            q = jnp.concatenate([query[(n, *at)].reshape(128, HD) for n in range(2)], axis=0)
            scores = lax.dot_general(q, keys, (((1,), (1,)), ((), ())), preferred_element_type=jnp.float32)
            picks = route[at].reshape(128, 128)
            gates = gate[at].reshape(128, 128)
            token = lax.broadcasted_iota(jnp.int32, (128, 640), 0) + (xa * 256 + half * 128)
            index = lax.broadcasted_iota(jnp.int32, (128, 640), 1) + ((xa - 2) * 256 + half * 128)
            allowed = (index <= token) & (index >= picks[:, 2:3].astype(jnp.int32))
            results = []
            for n in range(2):
                score = jnp.where(allowed, scores[n * 128 : n * 128 + 128], -1e30)
                shifted = jnp.exp(score - jnp.max(score, axis=1, keepdims=True))
                total = jnp.sum(shifted, axis=1, keepdims=True)
                mean = jnp.dot(shifted.astype(jnp.bfloat16), values, preferred_element_type=jnp.float32) / total
                results.append(mean * gates[:, n : n + 1])
            local = [picks[:, n : n + 1] - base.astype(jnp.float32) for n in range(2)]
            for e in range(EXPERTS):
                pair = jnp.where(local[0] == float(e), results[0], jnp.where(local[1] == float(e), results[1], 0.0))
                mixed[half * 128 : half * 128 + 128, e * HD : e * HD + HD] = pair.astype(jnp.bfloat16)
        for n in range(0, D, 512):
            made = jnp.dot(mixed[...], out_w[:, n : n + 512], preferred_element_type=jnp.float32)
            part[xa, :, :, n : n + 512] = made.astype(jnp.bfloat16).reshape(NZ, ROWS, 512)

    def update_cache():
        def page(p, _):
            content = pool[p].astype(jnp.float32)
            for b in range(8):
                rows = kv[parity, 2 + b // 2, pl.ds(b % 2 * 4, 4)].reshape(128, HD).astype(jnp.float32)
                hit = jnp.full((128, 128), pages[b] - p, jnp.int32) == 0
                content = jnp.where(hit, rows, content)
            pool[p] = content.astype(jnp.bfloat16)
            return 0

        lax.fori_loop(0, 16, page, 0)
        copy = pltpu.make_async_copy(pool, new_cache, store)
        copy.start()
        return copy

    def receive(task):
        half, i, j = task["block"]
        place = full.at[fz(j), fx(i), rows_of(half)]
        if task["deps"]:
            n = GATHER_KEYS.index(task["deps"][0])
            remote(place, place, gather_send.at[n], gather_recv.at[n], me).wait_recv()
        for link, key in task["sends"]:
            n = GATHER_KEYS.index(key)
            copy = remote(place, place, gather_send.at[n], gather_recv.at[n], links[link])
            copy.start()
            waiting.append(copy)

    def combine(task):
        half, i, j = task["block"]
        at = (fx(i), fz(j), rows_of(half))
        slots = [REDUCE_KEYS.index(key) for key in task["deps"]]
        for n in slots:
            remote(landed.at[n], landed.at[n], reduce_send.at[n], reduce_recv.at[n], me).wait_recv()
        if slots:
            total = part[at].astype(jnp.float32)
            for n in slots:
                total = total + landed[n].astype(jnp.float32)
            if not task["sends"]:
                total = total + hidden[rows_of(half), :].astype(jnp.float32)
                out[rows_of(half), :] = total.astype(jnp.bfloat16)
            else:
                part[at] = total.astype(jnp.bfloat16)
        for link, key in task["sends"]:
            n = REDUCE_KEYS.index(key)
            copy = remote(part.at[at], landed.at[n], reduce_send.at[n], reduce_recv.at[n], links[link])
            copy.start()
            waiting.append(copy)

    stored = None
    for task in plan()[0]:
        kind, *rest = task["name"]
        if kind == "recv":
            receive(task)
        elif kind == "sum":
            combine(task)
        elif kind == "cache":
            stored = update_cache()
        else:
            dict(norm=norm, setup=setup, project=project, swap=swap, attend=attend)[kind](*rest)
    for copy in waiting:
        copy.wait_send()
    stored.wait()


def local(hidden, gain, router, kv_weight, query_weight, out_weight, routes, segments, pages, cache):
    half = HD // 2
    frequency = (10000.0 ** (-np.arange(half, dtype=np.float32) / np.float32(half))).astype(np.float32)
    frequency = np.concatenate([frequency, frequency])[None]
    vmem = pl.BlockSpec(memory_space=pltpu.VMEM)
    anywhere = pl.BlockSpec(memory_space=pl.ANY)
    dma = pltpu.SemaphoreType.DMA
    return pl.pallas_call(
        layer,
        out_shape=(
            jax.ShapeDtypeStruct(hidden.shape, jnp.bfloat16),
            jax.ShapeDtypeStruct(cache.shape, jnp.bfloat16),
        ),
        in_specs=[vmem] * 3 + [anywhere] * 3 + [vmem] * 3 + [pl.BlockSpec(memory_space=pltpu.SMEM), anywhere],
        out_specs=(vmem, anywhere),
        scratch_shapes=[
            pltpu.VMEM((NZ, NX, ROWS, D), jnp.bfloat16),
            pltpu.VMEM((NX, NZ, ROWS, D), jnp.bfloat16),
            pltpu.VMEM((len(REDUCE_KEYS), HALF, D), jnp.bfloat16),
            pltpu.VMEM((D, 768), jnp.bfloat16),
            pltpu.VMEM((512, D), jnp.bfloat16),
            pltpu.VMEM((16, 128, HD), jnp.bfloat16),
            pltpu.VMEM((2, NX + 2, NZ, ROWS, HD), jnp.bfloat16),
            pltpu.VMEM((2, NX, NZ, ROWS, HD), jnp.bfloat16),
            pltpu.VMEM((NX, NZ, ROWS, HD), jnp.float32),
            pltpu.VMEM((NX, NZ, ROWS, HD), jnp.float32),
            pltpu.VMEM((NX, NZ, ROWS, HD), jnp.float32),
            pltpu.VMEM((NX, NZ, ROWS, HD), jnp.float32),
            pltpu.VMEM((256, 512), jnp.bfloat16),
            dma((len(GATHER_KEYS),)),
            dma((len(GATHER_KEYS),)),
            dma((len(REDUCE_KEYS),)),
            dma((len(REDUCE_KEYS),)),
            dma((NZ,)),
            dma((NZ,)),
            dma((4,)),
            dma(()),
        ],
        compiler_params=pltpu.CompilerParams(
            collective_id=0, has_side_effects=True, vmem_limit_bytes=52 * 1024 * 1024
        ),
        name="layer",
    )(
        hidden, gain.reshape(1, D), router.T, kv_weight, query_weight, out_weight, routes.T,
        segments.reshape(1, -1), jnp.asarray(frequency), pages, cache,
    )


def solution(mesh):
    placed = (
        P(("dp", "tensor"), None),
        P(),
        P(),
        P(None, "tensor"),
        P(None, "tensor"),
        P("tensor", None),
        P("dp", None),
        P("dp"),
        P("dp"),
        P("dp", None, "tensor"),
    )
    return jax.shard_map(
        local,
        mesh=mesh,
        in_specs=placed,
        out_specs=(P(("dp", "tensor"), None), P("dp", None, "tensor")),
        check_vma=False,
    )
```

```python
import functools

import jax
import jax.numpy as jnp
import numpy as np
from jax import lax
from jax.experimental import pallas as pl
from jax.experimental.pallas import tpu as pltpu
from jax.sharding import PartitionSpec as P

NX, NZ, ROWS, D, HD = 4, 8, 32, 2048, 128
EXPERTS = 4
GATHER_CUT, REDUCE_CUT = 768, 896
X_OFFSETS = (0, -1, 1, -2)
Z_OFFSETS = (0, -1, 1, -2, 2, -3, 3, -4)
GROUPS = ((0,), (-1, 1), (-2, 2), (-3, 3), (-4,))
LINK_BYTES_PER_US, LATENCY_US = 86600.0, 2.3


def gather_tasks():
    tasks = []
    for half in "AB":
        for i in X_OFFSETS:
            for j in Z_OFFSETS:
                sends = []
                if half == "A":
                    if j == 0 and i in (0, -1):
                        sends.append(("x+", (half, i - 1, 0)))
                    if j == 0 and i == 0:
                        sends.append(("x-", (half, 1, 0)))
                if -4 < j <= 0 and (half == "A" or i == 0):
                    sends.append(("z+", (half, i, j - 1)))
                if 0 <= j < 3 and (half == "A" or i == 0):
                    sends.append(("z-", (half, i, j + 1)))
                if half == "B":
                    if i in (0, -1):
                        sends.append(("x+", (half, i - 1, j)))
                    if i == 0:
                        sends.append(("x-", (half, 1, j)))
                own = i == 0 and j == 0
                tasks.append(
                    dict(
                        name=("recv", half, i, j),
                        deps=[] if own else [(half, i, j)],
                        after=[("norm",)] if own else [],
                        sends=sends,
                        block=(half, i, j),
                        cost=0.05,
                    )
                )
    return tasks


def reduce_tasks():
    tasks = []

    def add(half, i, j, deps, sends, cost):
        tasks.append(
            dict(name=("sum", half, i, j, len(tasks)), deps=deps, after=[("attend", i)], sends=sends, block=(half, i, j), cost=cost)
        )

    for i in (2, -1, 1, 0):
        for k in (4, 3, 2, 1):
            add("A", i, k, [("A", "L", i, k)] if k < 4 else [], [("z+", ("A", "L", i, k - 1))], 0.1)
        for k in (-3, -2, -1):
            add("A", i, k, [("A", "S", i, k)] if k > -3 else [], [("z-", ("A", "S", i, k + 1))], 0.1)
        deps = [("A", "L", i, 0), ("A", "S", i, 0)]
        if i == 1:
            deps.append(("A", "X", 1))
        if i == 0:
            deps += [("A", "X", 0), ("A", "Y", 0)]
        sends = {2: [("x+", ("A", "X", 1))], -1: [("x-", ("A", "Y", 0))], 1: [("x+", ("A", "X", 0))], 0: []}[i]
        add("A", i, 0, deps, sends, 0.15)
    for j in (4, -3, 3, -2, 2, -1, 1, 0):
        add("B", 2, j, [], [("x+", ("B", "L", 1, j))], 0.1)
        add("B", -1, j, [], [("x-", ("B", "S", 0, j))], 0.1)
        add("B", 1, j, [("B", "L", 1, j)], [("x+", ("B", "L", 0, j))], 0.1)
        deps = [("B", "L", 0, j), ("B", "S", 0, j)]
        sends = []
        if j > 0:
            deps += [("B", "Z", j)] if j < 4 else []
            sends = [("z+", ("B", "Z", j - 1))]
        elif j < 0:
            deps += [("B", "W", j)] if j > -3 else []
            sends = [("z-", ("B", "W", j + 1))]
        else:
            deps += [("B", "Z", 0), ("B", "W", 0)]
        add("B", 0, j, deps, sends, 0.15)
    return tasks


def compute_tasks():
    tasks = [dict(name=("norm",), after=[], cost=2.0)]
    tasks += [dict(name=("setup", n), after=[], cost=0.8) for n in range(4)]
    for group in GROUPS:
        after = [("recv", half, i, j) for half in "AB" for i in X_OFFSETS for j in group] + [("setup", n) for n in range(4)]
        tasks.append(dict(name=("project", *group), after=after, cost=0.1 + 0.7 * len(group)))
    everything = [("project", *group) for group in GROUPS]
    tasks.append(dict(name=("swap",), after=everything, cost=1.5))
    for i in (2, -1, 1, 0):
        tasks.append(dict(name=("attend", i), after=[("swap",)], cost=2.0))
    tasks.append(dict(name=("cache",), after=[("swap",), ("attend", 0)], cost=1.0))
    return tasks


@functools.cache
def plan():
    moves, work = gather_tasks() + reduce_tasks(), compute_tasks()
    clock, done, arrived, free, order = 0.0, set(), {}, {}, []
    while moves or work:
        best = None
        for task in moves:
            if all(a in done for a in task["after"]) and all(d in arrived for d in task["deps"]):
                at = max([arrived[d] for d in task["deps"]], default=0.0)
                if best is None or at < best[0]:
                    best = (at, task)
        ready = best is not None and best[0] <= clock
        task = None
        if not ready:
            task = next((w for w in work if all(a in done for a in w["after"])), None)
        if task is None:
            clock, task = max(clock, best[0]), best[1]
            moves.remove(task)
        else:
            work.remove(task)
        clock += task["cost"]
        for link, key in task.get("sends", []):
            cut = GATHER_CUT if len(key) == 3 and not isinstance(key[1], str) else REDUCE_CUT
            columns = cut if key[0] == "A" else D - cut
            free[link[0]] = max(clock, free.get(link[0], 0.0)) + ROWS * columns * 2 / LINK_BYTES_PER_US
            arrived[key] = free[link[0]] + LATENCY_US
        done.add(task["name"])
        order.append(task)
    return order, clock


FREQUENCY = [float(f) for f in (10000.0 ** (-np.arange(64, dtype=np.float32) / np.float32(64))).astype(np.float32)]
GATHER_KEYS = [t["block"] for t in gather_tasks() if t["deps"]]
REDUCE_KEYS = [key for t in reduce_tasks() for _, key in t["sends"]]
REDUCE_KEYS.sort(key=lambda key: key[0])
A_SLOTS = sum(key[0] == "A" for key in REDUCE_KEYS)


def layer(
    hidden_at, gain_at, router_at, kv_weight, query_weight, out_weight, routes_at, segments_at, pages_at, cache,
    out, pool,
    hidden, gain, router, routes, segments, pages,
    full, part, landed_a, landed_b, weight, out_w, kv, query, cosine, sine, route, gate, mixed,
    gather_send, gather_recv, reduce_send, reduce_recv, kv_send, kv_recv, load,
):
    me = lax.axis_index("tensor")
    turn = 1 - 2 * lax.rem(lax.axis_index("dp"), 2)
    x, z = me // NZ, lax.rem(me, NZ)
    parity = lax.rem(z, 2)
    base = parity * EXPERTS

    def fx(i):
        return lax.rem(x + turn * i + NX, NX)

    def fz(j):
        return lax.rem(z + turn * j + NZ, NZ)

    links = {
        "x+": fx(1) * NZ + z,
        "x-": fx(-1) * NZ + z,
        "z+": x * NZ + fz(1),
        "z-": x * NZ + fz(-1),
    }
    partner = x * NZ + z + 1 - 2 * parity

    barrier = pltpu.get_barrier_semaphore()
    for device in links.values():
        pl.semaphore_signal(barrier, inc=1, device_id={"tensor": device}, device_id_type=pl.DeviceIdType.MESH)

    early = [
        pltpu.make_async_copy(src, dst, load.at[4 + n])
        for n, (src, dst) in enumerate(
            [(hidden_at, hidden), (gain_at, gain), (router_at, router), (routes_at, routes), (segments_at, segments), (pages_at, pages)]
        )
    ]
    for copy in early:
        copy.start()
    loads = [
        pltpu.make_async_copy(query_weight, weight.at[:, 0:512], load.at[0]),
        pltpu.make_async_copy(kv_weight, weight.at[:, 512:640], load.at[1]),
        pltpu.make_async_copy(out_weight, out_w, load.at[2]),
        pltpu.make_async_copy(cache, pool, load.at[3]),
    ]
    for copy in loads:
        copy.start()

    def columns_of(half, cut):
        return pl.ds(0, cut) if half == "A" else pl.ds(cut, D - cut)

    def remote(src, dst, send, recv, device):
        return pltpu.make_async_remote_copy(
            src_ref=src, dst_ref=dst, send_sem=send, recv_sem=recv,
            device_id={"tensor": device}, device_id_type=pl.DeviceIdType.MESH,
        )

    lane = lax.broadcasted_iota(jnp.int32, (128, 128), 1)
    sub = lax.broadcasted_iota(jnp.int32, (128, 128), 0)
    low = lane < HD // 2
    waiting = []

    def norm():
        for copy in early[:2]:
            copy.wait()
        values = hidden[...].astype(jnp.float32)
        factor = lax.rsqrt(jnp.mean(values * values, axis=-1, keepdims=True) + 1e-05)
        gains = gain[...].astype(jnp.float32)
        for c in range(D // 128):
            at = slice(c * 128, c * 128 + 128)
            full[z, x, :, at] = (values[:, at] * factor * gains[c : c + 1]).astype(jnp.bfloat16)
        pl.semaphore_wait(barrier, 4)

    def setup(n):
        if n == 0:
            for copy in early[2:]:
                copy.wait()
        seg = segments[...]
        frequency = jnp.zeros((1, 128), jnp.float32)
        for f, value in enumerate(FREQUENCY):
            frequency = jnp.where(lax.rem(lane[0:1], HD // 2) == f, value, frequency)
        starts = [jnp.sum((seg < s).astype(jnp.float32), axis=1, keepdims=True) for s in (1, 2, 3)]
        for b in (2 * n, 2 * n + 1):
            token = (sub + b * 128).astype(jnp.float32)
            start = jnp.zeros_like(token)
            for s in starts:
                start = jnp.maximum(start, jnp.where(token >= s, s, 0.0))
            first = routes[0:1, b * 128 : b * 128 + 128].astype(jnp.float32)
            second = routes[1:2, b * 128 : b * 128 + 128].astype(jnp.float32)
            columns = jnp.where(sub == 0, first, jnp.where(sub == 1, second, 0.0)).T
            at = (b // 2, pl.ds(b % 2 * 4, 4))
            route[at] = jnp.where(lane == 2, start, columns).reshape(4, 32, 128)
            angle = (token - start) * frequency
            k = jnp.floor(angle * 0.6366197723675814 + 0.5)
            r = angle - k * 1.5703125
            r = r - k * 4.837512969970703e-4
            r = r - k * 7.549789954891882e-8
            w = r * r
            sin = r + r * w * (-1.6666654611e-1 + w * (8.3321608736e-3 - w * 1.9515295891e-4))
            cos = 1.0 - 0.5 * w + w * w * (4.166664568298827e-2 + w * (-1.388731625493765e-3 + w * 2.443315711809948e-5))
            quarter = k - 4.0 * jnp.floor(k * 0.25)
            odd = (quarter == 1.0) | (quarter == 3.0)
            c = jnp.where(odd, sin, cos)
            s = jnp.where(odd, cos, sin)
            c = jnp.where((quarter == 1.0) | (quarter == 2.0), -c, c)
            s = jnp.where(quarter >= 2.0, -s, s)
            cosine[at] = c.reshape(4, 32, 128)
            sine[at] = jnp.where(low, -s, s).reshape(4, 32, 128)
        for c in range(4 * n, 4 * n + 4):
            block = router[:, c * 128 : c * 128 + 128].astype(jnp.float32)
            block = jnp.concatenate([block, jnp.zeros((120, 128), jnp.float32)], axis=0)
            weight[c * 128 : c * 128 + 128, 640:768] = block.T.astype(jnp.bfloat16)
        if n == 0:
            kv[:, 0:2] = jnp.zeros((2, 2, NZ, ROWS, HD), jnp.bfloat16)
        if n == 3:
            for copy in loads:
                copy.wait()

    def rotate(values, c, s):
        return values * c + pltpu.roll(values, HD // 2, 1) * s

    def project(*group):
        rows = [full[fz(j)].reshape(128, D) for j in group]
        rows = rows[0] if len(group) == 1 else jnp.concatenate(rows, axis=0)
        made = jnp.dot(rows, weight[...], preferred_element_type=jnp.float32)
        for n, j in enumerate(group):
            place(j, made[n * 128 : n * 128 + 128])

    def place(j, made):
        za = fz(j)
        at = (slice(None), pl.ds(za, 1))
        picks = route[at].reshape(128, 128)
        c, s = cosine[at].reshape(128, 128), sine[at].reshape(128, 128)
        for n in range(2):
            local = picks[:, n : n + 1] - base.astype(jnp.float32)
            values = jnp.zeros((128, HD), jnp.float32)
            for e in range(EXPERTS):
                values = jnp.where(local == float(e), made[:, e * HD : e * HD + HD], values)
            values = rotate(values, c, s) * (HD**-0.5)
            query[(n, *at)] = values.astype(jnp.bfloat16).reshape(4, 1, 32, 128)
        own = made[:, 512:640]
        own = jnp.where(parity == 0, rotate(own, c, s), own)
        kv[parity, 2:6, pl.ds(za, 1)] = own.astype(jnp.bfloat16).reshape(4, 1, 32, 128)
        logits = made[:, 640:768]
        lanes = lane.astype(jnp.float32)
        first = jnp.sum(jnp.where(lanes == picks[:, 0:1], logits, 0.0), axis=1, keepdims=True)
        second = jnp.sum(jnp.where(lanes == picks[:, 1:2], logits, 0.0), axis=1, keepdims=True)
        top = jnp.maximum(first, second)
        first, second = jnp.exp(first - top), jnp.exp(second - top)
        total = first + second
        gate[at] = jnp.where(lane == 0, first / total, second / total).reshape(4, 1, 32, 128)
        rows = kv.at[parity, 2:6, za]
        copy = remote(rows, rows, kv_send.at[j % NZ], kv_recv.at[j % NZ], partner)
        copy.start()
        waiting.append(copy)

    def swap():
        for j in Z_OFFSETS:
            zp = lax.rem(z + 1 - 2 * parity + turn * j + NZ, NZ)
            place = kv.at[1 - parity, 2:6, zp]
            remote(place, place, kv_send.at[j % NZ], kv_recv.at[j % NZ], partner).wait_recv()

    def attend(i):
        xa = fx(i)
        for half in range(2):
            at = (xa, pl.ds(half * 4, 4))
            keys = kv[0, pl.ds(xa, 3)].reshape(768, HD)[half * 128 : half * 128 + 640]
            values = kv[1, pl.ds(xa, 3)].reshape(768, HD)[half * 128 : half * 128 + 640]
            q = jnp.concatenate([query[(n, *at)].reshape(128, HD) for n in range(2)], axis=0)
            scores = lax.dot_general(q, keys, (((1,), (1,)), ((), ())), preferred_element_type=jnp.float32)
            picks = route[at].reshape(128, 128)
            gates = gate[at].reshape(128, 128)
            token = lax.broadcasted_iota(jnp.int32, (128, 640), 0) + (xa * 256 + half * 128)
            index = lax.broadcasted_iota(jnp.int32, (128, 640), 1) + ((xa - 2) * 256 + half * 128)
            allowed = (index <= token) & (index >= picks[:, 2:3].astype(jnp.int32))
            results = []
            for n in range(2):
                score = jnp.where(allowed, scores[n * 128 : n * 128 + 128], -1e30)
                shifted = jnp.exp(score - jnp.max(score, axis=1, keepdims=True))
                total = jnp.sum(shifted, axis=1, keepdims=True)
                mean = jnp.dot(shifted.astype(jnp.bfloat16), values, preferred_element_type=jnp.float32) / total
                results.append(mean * gates[:, n : n + 1])
            local = [picks[:, n : n + 1] - base.astype(jnp.float32) for n in range(2)]
            for e in range(EXPERTS):
                pair = jnp.where(local[0] == float(e), results[0], jnp.where(local[1] == float(e), results[1], 0.0))
                mixed[half * 128 : half * 128 + 128, e * HD : e * HD + HD] = pair.astype(jnp.bfloat16)
        for n in range(0, D, 512):
            made = jnp.dot(mixed[...], out_w[:, n : n + 512], preferred_element_type=jnp.float32)
            part[xa, :, :, n : n + 512] = made.astype(jnp.bfloat16).reshape(NZ, ROWS, 512)

    def update_cache():
        def page(p, _):
            content = pool[p].astype(jnp.float32)
            for b in range(8):
                rows = kv[parity, 2 + b // 2, pl.ds(b % 2 * 4, 4)].reshape(128, HD).astype(jnp.float32)
                hit = jnp.full((128, 128), pages[b] - p, jnp.int32) == 0
                content = jnp.where(hit, rows, content)
            pool[p] = content.astype(jnp.bfloat16)
            return 0

        lax.fori_loop(0, 16, page, 0)

    def receive(task):
        half, i, j = task["block"]
        place = full.at[fz(j), fx(i), :, columns_of(half, GATHER_CUT)]
        if task["deps"]:
            n = GATHER_KEYS.index(task["deps"][0])
            remote(place, place, gather_send.at[n], gather_recv.at[n], me).wait_recv()
        for link, key in task["sends"]:
            n = GATHER_KEYS.index(key)
            copy = remote(place, place, gather_send.at[n], gather_recv.at[n], links[link])
            copy.start()
            waiting.append(copy)

    def combine(task):
        half, i, j = task["block"]
        columns = columns_of(half, REDUCE_CUT)
        at = (fx(i), fz(j), slice(None), columns)

        def landed(n):
            return landed_a.at[n] if half == "A" else landed_b.at[n - A_SLOTS]

        slots = [REDUCE_KEYS.index(key) for key in task["deps"]]
        for n in slots:
            remote(landed(n), landed(n), reduce_send.at[n], reduce_recv.at[n], me).wait_recv()
        if slots:
            total = part[at].astype(jnp.float32)
            for n in slots:
                total = total + landed(n)[...].astype(jnp.float32)
            if not task["sends"]:
                total = total + hidden[:, columns].astype(jnp.float32)
                out[:, columns] = total.astype(jnp.bfloat16)
            else:
                part[at] = total.astype(jnp.bfloat16)
        for link, key in task["sends"]:
            n = REDUCE_KEYS.index(key)
            copy = remote(part.at[at], landed(n), reduce_send.at[n], reduce_recv.at[n], links[link])
            copy.start()
            waiting.append(copy)

    for task in plan()[0]:
        kind, *rest = task["name"]
        if kind == "recv":
            receive(task)
        elif kind == "sum":
            combine(task)
        elif kind == "cache":
            update_cache()
        else:
            dict(norm=norm, setup=setup, project=project, swap=swap, attend=attend)[kind](*rest)
    for copy in waiting:
        copy.wait_send()


def local(hidden, gain, router, kv_weight, query_weight, out_weight, routes, segments, pages, cache):
    vmem, hbm = pl.BlockSpec(memory_space=pltpu.VMEM), pl.BlockSpec(memory_space=pltpu.HBM)
    dma = pltpu.SemaphoreType.DMA
    return pl.pallas_call(
        layer,
        out_shape=(
            jax.ShapeDtypeStruct(hidden.shape, jnp.bfloat16),
            jax.ShapeDtypeStruct(cache.shape, jnp.bfloat16),
        ),
        in_specs=[hbm] * 10,
        out_specs=(vmem, vmem),
        scratch_shapes=[
            pltpu.VMEM((ROWS, D), jnp.bfloat16),
            pltpu.VMEM((D // 128, 128), jnp.bfloat16),
            pltpu.VMEM((8, D), jnp.bfloat16),
            pltpu.VMEM((2, 1024), jnp.int32),
            pltpu.VMEM((1, 1024), jnp.int32),
            pltpu.SMEM((8,), jnp.int32),
            pltpu.VMEM((NZ, NX, ROWS, D), jnp.bfloat16),
            pltpu.VMEM((NX, NZ, ROWS, D), jnp.bfloat16),
            pltpu.VMEM((A_SLOTS, ROWS, REDUCE_CUT), jnp.bfloat16),
            pltpu.VMEM((len(REDUCE_KEYS) - A_SLOTS, ROWS, D - REDUCE_CUT), jnp.bfloat16),
            pltpu.VMEM((D, 768), jnp.bfloat16),
            pltpu.VMEM((512, D), jnp.bfloat16),
            pltpu.VMEM((2, NX + 2, NZ, ROWS, HD), jnp.bfloat16),
            pltpu.VMEM((2, NX, NZ, ROWS, HD), jnp.bfloat16),
            pltpu.VMEM((NX, NZ, ROWS, HD), jnp.float32),
            pltpu.VMEM((NX, NZ, ROWS, HD), jnp.float32),
            pltpu.VMEM((NX, NZ, ROWS, HD), jnp.float32),
            pltpu.VMEM((NX, NZ, ROWS, HD), jnp.float32),
            pltpu.VMEM((256, 512), jnp.bfloat16),
            dma((len(GATHER_KEYS),)),
            dma((len(GATHER_KEYS),)),
            dma((len(REDUCE_KEYS),)),
            dma((len(REDUCE_KEYS),)),
            dma((NZ,)),
            dma((NZ,)),
            dma((10,)),
        ],
        compiler_params=pltpu.CompilerParams(
            collective_id=0, has_side_effects=True, vmem_limit_bytes=63 * 1024 * 1024
        ),
        name="layer",
    )(
        hidden, gain.reshape(D // 128, 128), router.T, kv_weight, query_weight, out_weight, routes.T,
        segments.reshape(1, -1), pages, cache,
    )


def solution(mesh):
    placed = (
        P(("dp", "tensor"), None),
        P(),
        P(),
        P(None, "tensor"),
        P(None, "tensor"),
        P("tensor", None),
        P("dp", None),
        P("dp"),
        P("dp"),
        P("dp", None, "tensor"),
    )
    return jax.shard_map(
        local,
        mesh=mesh,
        in_specs=placed,
        out_specs=(P(("dp", "tensor"), None), P("dp", None, "tensor")),
        check_vma=False,
    )
```

```python
import functools

import jax
import jax.numpy as jnp
import numpy as np
from jax import lax
from jax.experimental import pallas as pl
from jax.experimental.pallas import tpu as pltpu
from jax.sharding import PartitionSpec as P

NX, NZ, ROWS, D, HD = 4, 8, 32, 2048, 128
EXPERTS = 4
GATHER_CUT, REDUCE_CUT = 768, 896
Z_OFFSETS = (0, 1, 7, 2, 6, 3, 5, 4)
GROUPS = ((0,), (1, 7), (2, 6), (3, 5), (4,))
ATTEND_ORDER = (2, 1, 3, 0)
GATHER_CUT, REDUCE_CUT = 768, 896
LINK_BYTES_PER_US, LATENCY_US = 43000.0, 2.1
FREQUENCY = [float(f) for f in (10000.0 ** (-np.arange(64, dtype=np.float32) / np.float32(64))).astype(np.float32)]

RING4 = {0: (1, -1), 1: (2,)}
CHAIN8 = {0: (1, -1), 1: (2,), 2: (3,), 3: (4,), -1: (-2,), -2: (-3,)}
SKIP8 = {0: (1, 2, -1), 2: (3,), 3: (4,), -1: (-2,), -2: (-3,)}
WIDE8 = {0: (1, -1, 2, -2), 2: (3, 4), -2: (-3,)}


def turned(tree, n, sign):
    return {sign * p % n: tuple(sign * q % n for q in rest) for p, rest in tree.items()}


def x_tree(half, pz):
    return turned(RING4, NX, 1 if half == "A" or pz % 2 else -1)


def z_tree(phase, half, px):
    if half == "A":
        return turned(CHAIN8, NZ, 1 if px < 2 else -1)
    return turned(SKIP8 if phase == "gather" else WIDE8, NZ, -1)


def children(phase, half, px, pz):
    found = []
    if half == "B" or pz == 0:
        found += [(q, pz) for q in x_tree(half, pz).get(px, ())]
    if half == "A" or px == 0:
        found += [(px, q) for q in z_tree(phase, half, px).get(pz, ())]
    return found


def parent(phase, half, px, pz):
    places = [(i, j) for i in range(NX) for j in range(NZ)]
    return next((p for p in places if (px, pz) in children(phase, half, *p)), None)


def links_of(one, other):
    dx, dz = (other[0] - one[0]) % NX, (other[1] - one[1]) % NZ
    if dx:
        return ("x+", 1) if dx == 1 else ("x-", 1)
    return ("z+", dz) if dz < 4 else ("z-", NZ - dz)


def move_tasks():
    tasks = []
    for half in "AB":
        for px in range(NX):
            for pz in range(NZ):
                own = (px, pz) == (0, 0)
                here = ("gather", half, px, pz)
                sends = [((px, pz), q, ("gather", half, *q)) for q in children(*here)]
                tasks.append(dict(name=here, deps=[] if own else [here], after=[("norm",)] if own else [], sends=sends, cost=0.06))
    for half in "AB":
        for px in ATTEND_ORDER:
            for pz in range(NZ):
                here = ("reduce", half, px, pz)
                deps = [("reduce", half, *q) for q in children(*here)]
                up = parent(*here)
                sends = [((px, pz), up, here)] if up else []
                tasks.append(dict(name=here, deps=deps, after=[("attend", px)], sends=sends, cost=0.06))
    return tasks


def compute_tasks():
    tasks = [dict(name=("norm",), after=[], cost=2.0)]
    tasks += [dict(name=("setup", n), after=[], cost=0.6) for n in range(4)]
    for group in GROUPS:
        after = [("gather", half, i, j) for half in "AB" for i in range(NX) for j in group] + [("setup", n) for n in range(4)]
        tasks.append(dict(name=("project", *group), after=after, cost=0.25 + 0.75 * len(group)))
    everything = [("project", *group) for group in GROUPS]
    tasks.append(dict(name=("swap",), after=everything, cost=2.5))
    for i in ATTEND_ORDER:
        tasks.append(dict(name=("attend", i), after=[("swap",)], cost=1.75))
    tasks.append(dict(name=("cache",), after=[("swap",), ("attend", ATTEND_ORDER[-1])], cost=1.0))
    return tasks


def columns_in(phase, half):
    cut = GATHER_CUT if phase == "gather" else REDUCE_CUT
    return (0, cut) if half == "A" else (cut, D - cut)


@functools.cache
def plan():
    moves, work = move_tasks(), compute_tasks()
    clock, done, arrived, free, order = 0.0, set(), {}, {}, []
    while moves or work:
        best = None
        for task in moves:
            if all(a in done for a in task["after"]) and all(d in arrived for d in task["deps"]):
                at = max([arrived[d] for d in task["deps"]], default=0.0)
                if best is None or at < best[0]:
                    best = (at, task)
        task = None
        if best is None or best[0] > clock:
            task = next((w for w in work if all(a in done for a in w["after"])), None)
        if task is None:
            clock, task = max(clock, best[0]), best[1]
            moves.remove(task)
        else:
            work.remove(task)
        clock += task["cost"]
        for one, other, key in task.get("sends", []):
            link, hops = links_of(one, other)
            took = ROWS * columns_in(*key[:2])[1] * 2 / LINK_BYTES_PER_US
            free[link] = max(clock, free.get(link, 0.0)) + took * hops
            arrived[key] = free[link] - took * (hops - 1) + LATENCY_US
        done.add(task["name"])
        order.append(task)
    return order, clock


def slot(half, px, pz):
    return px * NZ + pz - 1


SLOTS = NX * NZ - 1


def layer(
    hidden_at, gain_at, router_at, kv_weight, query_weight, out_weight, routes_at, segments_at, pages_at, cache,
    out, pool,
    hidden, gain, router, routes, segments, pages,
    full, part, landed_a, landed_b, weight, out_w, kv, query, cosine, sine, route, gate, mixed,
    gather_send, gather_recv, reduce_send, reduce_recv, kv_send, kv_recv, load,
):
    me = lax.axis_index("tensor")
    turn = 1 - 2 * lax.rem(lax.axis_index("dp"), 2)
    x, z = me // NZ, lax.rem(me, NZ)
    parity = lax.rem(z, 2)
    base = parity * EXPERTS

    def fx(px):
        return lax.rem(x - turn * px + 2 * NX, NX)

    def fz(pz):
        return lax.rem(z - turn * pz + 2 * NZ, NZ)

    def device_at(one, other):
        return fx(one[0] - other[0]) * NZ + fz(one[1] - other[1])

    near = [device_at((0, 0), p) for p in ((1, 0), (-1, 0), (0, 1), (0, -1), (0, 2), (0, -2))]
    partner = x * NZ + z + 1 - 2 * parity

    barrier = pltpu.get_barrier_semaphore()
    for device in near:
        pl.semaphore_signal(barrier, inc=1, device_id={"tensor": device}, device_id_type=pl.DeviceIdType.MESH)

    early = [
        pltpu.make_async_copy(src, dst, load.at[4 + n])
        for n, (src, dst) in enumerate(
            [(hidden_at, hidden), (gain_at, gain), (router_at, router), (routes_at, routes), (segments_at, segments), (pages_at, pages)]
        )
    ]
    for copy in early:
        copy.start()
    loads = [
        pltpu.make_async_copy(query_weight, weight.at[:, 0:512], load.at[0]),
        pltpu.make_async_copy(kv_weight, weight.at[:, 512:640], load.at[1]),
        pltpu.make_async_copy(out_weight, out_w, load.at[2]),
        pltpu.make_async_copy(cache, pool, load.at[3]),
    ]
    for copy in loads:
        copy.start()

    def columns_of(phase, half):
        return pl.ds(*columns_in(phase, half))

    def remote(src, dst, send, recv, device):
        return pltpu.make_async_remote_copy(
            src_ref=src, dst_ref=dst, send_sem=send, recv_sem=recv,
            device_id={"tensor": device}, device_id_type=pl.DeviceIdType.MESH,
        )

    lane = lax.broadcasted_iota(jnp.int32, (128, 128), 1)
    sub = lax.broadcasted_iota(jnp.int32, (128, 128), 0)
    low = lane < HD // 2
    waiting = []

    def norm():
        for copy in early[:2]:
            copy.wait()
        values = hidden[...].astype(jnp.float32)
        factor = lax.rsqrt(jnp.mean(values * values, axis=-1, keepdims=True) + 1e-05)
        gains = gain[...].astype(jnp.float32)
        for c in range(D // 128):
            at = slice(c * 128, c * 128 + 128)
            full[z, x, :, at] = (values[:, at] * factor * gains[c : c + 1]).astype(jnp.bfloat16)
        pl.semaphore_wait(barrier, len(near))

    def setup(n):
        if n == 0:
            for copy in early[2:]:
                copy.wait()
        seg = segments[...]
        frequency = jnp.zeros((1, 128), jnp.float32)
        for f, value in enumerate(FREQUENCY):
            frequency = jnp.where(lax.rem(lane[0:1], HD // 2) == f, value, frequency)
        starts = [jnp.sum((seg < s).astype(jnp.float32), axis=1, keepdims=True) for s in (1, 2, 3)]
        for b in (2 * n, 2 * n + 1):
            token = (sub + b * 128).astype(jnp.float32)
            start = jnp.zeros_like(token)
            for s in starts:
                start = jnp.maximum(start, jnp.where(token >= s, s, 0.0))
            first = routes[0:1, b * 128 : b * 128 + 128].astype(jnp.float32)
            second = routes[1:2, b * 128 : b * 128 + 128].astype(jnp.float32)
            columns = jnp.where(sub == 0, first, jnp.where(sub == 1, second, 0.0)).T
            at = (b // 2, pl.ds(b % 2 * 4, 4))
            route[at] = jnp.where(lane == 2, start, columns).reshape(4, 32, 128)
            angle = (token - start) * frequency
            k = jnp.floor(angle * 0.6366197723675814 + 0.5)
            r = angle - k * 1.5703125
            r = r - k * 4.837512969970703e-4
            r = r - k * 7.549789954891882e-8
            w = r * r
            sin = r + r * w * (-1.6666654611e-1 + w * (8.3321608736e-3 - w * 1.9515295891e-4))
            cos = 1.0 - 0.5 * w + w * w * (4.166664568298827e-2 + w * (-1.388731625493765e-3 + w * 2.443315711809948e-5))
            quarter = k - 4.0 * jnp.floor(k * 0.25)
            odd = (quarter == 1.0) | (quarter == 3.0)
            c = jnp.where(odd, sin, cos)
            s = jnp.where(odd, cos, sin)
            c = jnp.where((quarter == 1.0) | (quarter == 2.0), -c, c)
            s = jnp.where(quarter >= 2.0, -s, s)
            cosine[at] = c.reshape(4, 32, 128)
            sine[at] = jnp.where(low, -s, s).reshape(4, 32, 128)
        for c in range(4 * n, 4 * n + 4):
            block = router[:, c * 128 : c * 128 + 128].astype(jnp.float32)
            block = jnp.concatenate([block, jnp.zeros((120, 128), jnp.float32)], axis=0)
            weight[c * 128 : c * 128 + 128, 640:768] = block.T.astype(jnp.bfloat16)
        if n == 0:
            kv[:, 0:2] = jnp.zeros((2, 2, NZ, ROWS, HD), jnp.bfloat16)
        if n == 3:
            for copy in loads:
                copy.wait()

    def rotate(values, c, s):
        return values * c + pltpu.roll(values, HD // 2, 1) * s

    def project(*group):
        rows = [full[fz(j)].reshape(128, D) for j in group]
        rows = rows[0] if len(group) == 1 else jnp.concatenate(rows, axis=0)
        made = jnp.dot(rows, weight[:, 512:768], preferred_element_type=jnp.float32)
        for n, j in enumerate(group):
            place_kv(j, made[n * 128 : n * 128 + 128])
        made = jnp.dot(rows, weight[:, 0:512], preferred_element_type=jnp.float32)
        for n, j in enumerate(group):
            place_queries(j, made[n * 128 : n * 128 + 128])

    def place_queries(j, made):
        za = fz(j)
        at = (slice(None), pl.ds(za, 1))
        picks = route[at].reshape(128, 128)
        c, s = cosine[at].reshape(128, 128), sine[at].reshape(128, 128)
        for n in range(2):
            local = picks[:, n : n + 1] - base.astype(jnp.float32)
            values = jnp.zeros((128, HD), jnp.float32)
            for e in range(EXPERTS):
                values = jnp.where(local == float(e), made[:, e * HD : e * HD + HD], values)
            values = rotate(values, c, s) * (HD**-0.5)
            query[(n, *at)] = values.astype(jnp.bfloat16).reshape(4, 1, 32, 128)

    def place_kv(j, made):
        za = fz(j)
        at = (slice(None), pl.ds(za, 1))
        picks = route[at].reshape(128, 128)
        c, s = cosine[at].reshape(128, 128), sine[at].reshape(128, 128)
        own = made[:, 0:128]
        own = jnp.where(parity == 0, rotate(own, c, s), own)
        kv[parity, 2:6, pl.ds(za, 1)] = own.astype(jnp.bfloat16).reshape(4, 1, 32, 128)
        rows = kv.at[parity, 2:6, za]
        copy = remote(rows, rows, kv_send.at[j], kv_recv.at[j], partner)
        copy.start()
        waiting.append(copy)
        logits = made[:, 128:256]
        lanes = lane.astype(jnp.float32)
        first = jnp.sum(jnp.where(lanes == picks[:, 0:1], logits, 0.0), axis=1, keepdims=True)
        second = jnp.sum(jnp.where(lanes == picks[:, 1:2], logits, 0.0), axis=1, keepdims=True)
        top = jnp.maximum(first, second)
        first, second = jnp.exp(first - top), jnp.exp(second - top)
        total = first + second
        gate[at] = jnp.where(lane == 0, first / total, second / total).reshape(4, 1, 32, 128)

    def swap():
        for j in Z_OFFSETS:
            zp = lax.rem(z + 1 - 2 * parity - turn * j + 2 * NZ, NZ)
            place = kv.at[1 - parity, 2:6, zp]
            remote(place, place, kv_send.at[j], kv_recv.at[j], partner).wait_recv()

    def attend(i):
        xa = fx(i)
        for half in range(2):
            at = (xa, pl.ds(half * 4, 4))
            keys = kv[0, pl.ds(xa, 3)].reshape(768, HD)[half * 128 : half * 128 + 640]
            values = kv[1, pl.ds(xa, 3)].reshape(768, HD)[half * 128 : half * 128 + 640]
            q = jnp.concatenate([query[(n, *at)].reshape(128, HD) for n in range(2)], axis=0)
            scores = lax.dot_general(q, keys, (((1,), (1,)), ((), ())), preferred_element_type=jnp.float32)
            picks = route[at].reshape(128, 128)
            gates = gate[at].reshape(128, 128)
            token = lax.broadcasted_iota(jnp.int32, (128, 640), 0) + (xa * 256 + half * 128)
            index = lax.broadcasted_iota(jnp.int32, (128, 640), 1) + ((xa - 2) * 256 + half * 128)
            allowed = (index <= token) & (index >= picks[:, 2:3].astype(jnp.int32))
            results = []
            for n in range(2):
                score = jnp.where(allowed, scores[n * 128 : n * 128 + 128], -1e30)
                shifted = jnp.exp(score - jnp.max(score, axis=1, keepdims=True))
                total = jnp.sum(shifted, axis=1, keepdims=True)
                mean = jnp.dot(shifted.astype(jnp.bfloat16), values, preferred_element_type=jnp.float32) / total
                results.append(mean * gates[:, n : n + 1])
            local = [picks[:, n : n + 1] - base.astype(jnp.float32) for n in range(2)]
            for e in range(EXPERTS):
                pair = jnp.where(local[0] == float(e), results[0], jnp.where(local[1] == float(e), results[1], 0.0))
                mixed[half * 128 : half * 128 + 128, e * HD : e * HD + HD] = pair.astype(jnp.bfloat16)
        for n in range(0, D, 512):
            made = jnp.dot(mixed[...], out_w[:, n : n + 512], preferred_element_type=jnp.float32)
            part[xa, :, :, n : n + 512] = made.astype(jnp.bfloat16).reshape(NZ, ROWS, 512)

    def update_cache():
        def page(p, _):
            content = pool[p].astype(jnp.float32)
            for b in range(8):
                rows = kv[parity, 2 + b // 2, pl.ds(b % 2 * 4, 4)].reshape(128, HD).astype(jnp.float32)
                hit = jnp.full((128, 128), pages[b] - p, jnp.int32) == 0
                content = jnp.where(hit, rows, content)
            pool[p] = content.astype(jnp.bfloat16)
            return 0

        lax.fori_loop(0, 16, page, 0)

    def receive(half, px, pz, task):
        block = full.at[fz(pz), fx(px), :, columns_of("gather", half)]
        if task["deps"]:
            n = slot(half, px, pz)
            part_n = "AB".index(half)
            remote(block, block, gather_send.at[part_n, n], gather_recv.at[part_n, n], me).wait_recv()
        send(task, block, lambda n: block, gather_send, gather_recv)

    def send(task, src, dst, send_sem, recv_sem):
        for one, other, key in task["sends"]:
            part_n, n = "AB".index(key[1]), slot(*key[1:])
            copy = remote(src, dst(n), send_sem.at[part_n, n], recv_sem.at[part_n, n], device_at(one, other))
            copy.start()
            waiting.append(copy)

    def combine(half, px, pz, task):
        columns = columns_of("reduce", half)
        at = (fx(px), fz(pz), slice(None), columns)
        landed = landed_a if half == "A" else landed_b
        part_n = "AB".index(half)
        slots = [slot(*key[1:]) for key in task["deps"]]
        for n in slots:
            remote(landed.at[n], landed.at[n], reduce_send.at[part_n, n], reduce_recv.at[part_n, n], me).wait_recv()
        if slots:
            total = part[at].astype(jnp.float32)
            for n in slots:
                total = total + landed[n].astype(jnp.float32)
            if task["sends"]:
                part[at] = total.astype(jnp.bfloat16)
            else:
                out[:, columns] = (total + hidden[:, columns].astype(jnp.float32)).astype(jnp.bfloat16)
        send(task, part.at[at], lambda n: landed.at[n], reduce_send, reduce_recv)

    for task in plan()[0]:
        kind, *rest = task["name"]
        if kind == "gather":
            receive(*rest, task)
        elif kind == "reduce":
            combine(*rest, task)
        elif kind == "cache":
            update_cache()
        else:
            dict(norm=norm, setup=setup, project=project, swap=swap, attend=attend)[kind](*rest)
    for copy in waiting:
        copy.wait_send()


def local(hidden, gain, router, kv_weight, query_weight, out_weight, routes, segments, pages, cache):
    vmem, hbm = pl.BlockSpec(memory_space=pltpu.VMEM), pl.BlockSpec(memory_space=pltpu.HBM)
    dma = pltpu.SemaphoreType.DMA
    return pl.pallas_call(
        layer,
        out_shape=(
            pltpu.VMEM(hidden.shape, jnp.bfloat16),
            pltpu.VMEM(cache.shape, jnp.bfloat16),
        ),
        in_specs=[hbm] * 10,
        out_specs=(vmem, vmem),
        scratch_shapes=[
            pltpu.VMEM((ROWS, D), jnp.bfloat16),
            pltpu.VMEM((D // 128, 128), jnp.bfloat16),
            pltpu.VMEM((8, D), jnp.bfloat16),
            pltpu.VMEM((2, 1024), jnp.int32),
            pltpu.VMEM((1, 1024), jnp.int32),
            pltpu.SMEM((8,), jnp.int32),
            pltpu.VMEM((NZ, NX, ROWS, D), jnp.bfloat16),
            pltpu.VMEM((NX, NZ, ROWS, D), jnp.bfloat16),
            pltpu.VMEM((SLOTS, ROWS, REDUCE_CUT), jnp.bfloat16),
            pltpu.VMEM((SLOTS, ROWS, D - REDUCE_CUT), jnp.bfloat16),
            pltpu.VMEM((D, 768), jnp.bfloat16),
            pltpu.VMEM((512, D), jnp.bfloat16),
            pltpu.VMEM((2, NX + 2, NZ, ROWS, HD), jnp.bfloat16),
            pltpu.VMEM((2, NX, NZ, ROWS, HD), jnp.bfloat16),
            pltpu.VMEM((NX, NZ, ROWS, HD), jnp.float32),
            pltpu.VMEM((NX, NZ, ROWS, HD), jnp.float32),
            pltpu.VMEM((NX, NZ, ROWS, HD), jnp.float32),
            pltpu.VMEM((NX, NZ, ROWS, HD), jnp.float32),
            pltpu.VMEM((256, 512), jnp.bfloat16),
            dma((2, SLOTS)),
            dma((2, SLOTS)),
            dma((2, SLOTS)),
            dma((2, SLOTS)),
            dma((NZ,)),
            dma((NZ,)),
            dma((10,)),
        ],
        compiler_params=pltpu.CompilerParams(
            collective_id=0, has_side_effects=True, vmem_limit_bytes=62 * 1024 * 1024
        ),
        name="layer",
    )(
        hidden, gain.reshape(D // 128, 128), router.T, kv_weight, query_weight, out_weight, routes.T,
        segments.reshape(1, -1), pages, cache,
    )


def solution(mesh):
    placed = (
        P(("dp", "tensor"), None),
        P(),
        P(),
        P(None, "tensor"),
        P(None, "tensor"),
        P("tensor", None),
        P("dp", None),
        P("dp"),
        P("dp"),
        P("dp", None, "tensor"),
    )
    return jax.shard_map(
        local,
        mesh=mesh,
        in_specs=placed,
        out_specs=(P(("dp", "tensor"), None), P("dp", None, "tensor")),
        check_vma=False,
    )
```

```python
import functools

import jax
import jax.numpy as jnp
import numpy as np
from jax import lax
from jax.experimental import pallas as pl
from jax.experimental.pallas import tpu as pltpu
from jax.sharding import PartitionSpec as P

NX, NZ, ROWS, D, HD = 4, 8, 32, 2048, 128
EXPERTS = 4
Z_OFFSETS = (0, 1, 7, 2, 6, 3, 5, 4)
GROUPS = ((0,), (1, 7), (2, 6), (3, 5), (4,))
ATTEND_ORDER = (2, 1, 3, 0)
GATHER_CUT, REDUCE_CUT = 768, 896
PIECES = 1
PIECE = ROWS // PIECES
LINK_BYTES_PER_US, LATENCY_US = 43000.0, 3.0
FREQUENCY = [float(f) for f in (10000.0 ** (-np.arange(64, dtype=np.float32) / np.float32(64))).astype(np.float32)]

RING4 = {0: (1, -1), 1: (2,)}
CHAIN8 = {0: (1, -1), 1: (2,), 2: (3,), 3: (4,), -1: (-2,), -2: (-3,)}
SKIP8 = {0: (1, 2, -1), 2: (3,), 3: (4,), -1: (-2,), -2: (-3,)}
WIDE8 = {0: (1, -1, 2, -2), 2: (3, 4), -2: (-3,)}


def turned(tree, n, sign):
    return {sign * p % n: tuple(sign * q % n for q in rest) for p, rest in tree.items()}


def x_tree(half, pz):
    return turned(RING4, NX, 1 if half == "A" or pz % 2 else -1)


def z_tree(phase, half, px):
    if half == "A":
        return turned(CHAIN8, NZ, 1 if px < 2 else -1)
    return turned(SKIP8 if phase == "gather" else WIDE8, NZ, -1)


def children(phase, half, px, pz):
    found = []
    if half == "B" or pz == 0:
        found += [(q, pz) for q in x_tree(half, pz).get(px, ())]
    if half == "A" or px == 0:
        found += [(px, q) for q in z_tree(phase, half, px).get(pz, ())]
    return found


def parent(phase, half, px, pz):
    places = [(i, j) for i in range(NX) for j in range(NZ)]
    return next((p for p in places if (px, pz) in children(phase, half, *p)), None)


def links_of(one, other):
    dx, dz = (other[0] - one[0]) % NX, (other[1] - one[1]) % NZ
    if dx:
        return ("x+", 1) if dx == 1 else ("x-", 1)
    return ("z+", dz) if dz < 4 else ("z-", NZ - dz)


def move_tasks():
    tasks = []
    for half in "AB":
        for px in range(NX):
            for pz in range(NZ):
                for r in range(PIECES):
                    own = (px, pz) == (0, 0)
                    here = ("gather", half, px, pz, r)
                    sends = [((px, pz), q, ("gather", half, *q, r)) for q in children(*here[:4])]
                    tasks.append(
                        dict(name=here, deps=[] if own else [here], after=[("norm",)] if own else [], sends=sends, cost=0.06)
                    )
    for half in "AB":
        for px in ATTEND_ORDER:
            for pz in range(NZ):
                for r in range(PIECES):
                    here = ("reduce", half, px, pz, r)
                    deps = [("reduce", half, *q, r) for q in children(*here[:4])]
                    up = parent(*here[:4])
                    sends = [((px, pz), up, here)] if up else []
                    tasks.append(dict(name=here, deps=deps, after=[("attend", px)], sends=sends, cost=0.06))
    return tasks


def compute_tasks():
    tasks = [dict(name=("norm",), after=[], cost=2.0)]
    tasks += [dict(name=("setup", n), after=[], cost=0.6) for n in range(4)]
    for group in GROUPS:
        after = [("gather", half, i, j, r) for half in "AB" for i in range(NX) for j in group for r in range(PIECES)] + [("setup", n) for n in range(4)]
        tasks.append(dict(name=("project", *group), after=after, cost=0.25 + 0.75 * len(group)))
    everything = [("project", *group) for group in GROUPS]
    tasks.append(dict(name=("swap",), after=everything, cost=2.5))
    for i in ATTEND_ORDER:
        tasks.append(dict(name=("attend", i), after=[("swap",)], cost=1.75))
    tasks.append(dict(name=("cache",), after=[("swap",), ("attend", ATTEND_ORDER[-1])], cost=1.0))
    return tasks


def columns_in(phase, half):
    cut = GATHER_CUT if phase == "gather" else REDUCE_CUT
    return (0, cut) if half == "A" else (cut, D - cut)


@functools.cache
def plan():
    moves, work = move_tasks(), compute_tasks()
    clock, done, arrived, free, order = 0.0, set(), {}, {}, []
    while moves or work:
        best = None
        for task in moves:
            if all(a in done for a in task["after"]) and all(d in arrived for d in task["deps"]):
                at = max([arrived[d] for d in task["deps"]], default=0.0)
                if best is None or at < best[0]:
                    best = (at, task)
        task = None
        if best is None or best[0] > clock:
            task = next((w for w in work if all(a in done for a in w["after"])), None)
        if task is None:
            clock, task = max(clock, best[0]), best[1]
            moves.remove(task)
        else:
            work.remove(task)
        clock += task["cost"]
        for one, other, key in task.get("sends", []):
            link, hops = links_of(one, other)
            took = PIECE * columns_in(*key[:2])[1] * 2 / LINK_BYTES_PER_US
            free[link] = max(clock, free.get(link, 0.0)) + took * hops
            arrived[key] = free[link] - took * (hops - 1) + LATENCY_US
        done.add(task["name"])
        order.append(task)
    return order, clock


def slot(px, pz):
    return px * NZ + pz - 1


SLOTS = NX * NZ - 1


def layer(
    hidden_at, gain_at, router_at, kv_weight, query_weight, out_weight, routes_at, segments_at, pages_at, cache,
    out, pool,
    hidden, gain, router, routes, segments, pages,
    full, part, landed_a, landed_b, weight, out_w, kv, query, cosine, sine, route, gate, mixed,
    gather_send, gather_recv, reduce_send, reduce_recv, kv_send, kv_recv, load,
):
    me = lax.axis_index("tensor")
    turn = 1 - 2 * lax.rem(lax.axis_index("dp"), 2)
    x, z = me // NZ, lax.rem(me, NZ)
    parity = lax.rem(z, 2)
    base = parity * EXPERTS

    x_of = [lax.rem(x - turn * px + 2 * NX, NX) for px in range(NX)]
    z_of = [lax.rem(z - turn * pz + 2 * NZ, NZ) for pz in range(NZ)]
    x_steps, z_steps = [0] + [xo * NZ + z for xo in x_of[1:]], [x * NZ + zo for zo in z_of]

    def fx(px):
        return x_of[px % NX]

    def fz(pz):
        return z_of[pz % NZ]

    def device_at(one, other):
        dx, dz = (one[0] - other[0]) % NX, (one[1] - other[1]) % NZ
        return x_steps[dx] if dx else z_steps[dz]

    near = [device_at((0, 0), p) for p in ((1, 0), (-1, 0), (0, 1), (0, -1), (0, 2), (0, -2))]
    partner = x * NZ + z + 1 - 2 * parity

    barrier = pltpu.get_barrier_semaphore()
    for device in near:
        pl.semaphore_signal(barrier, inc=1, device_id={"tensor": device}, device_id_type=pl.DeviceIdType.MESH)

    early = [
        pltpu.make_async_copy(src, dst, load.at[4 + n])
        for n, (src, dst) in enumerate(
            [(hidden_at, hidden), (gain_at, gain), (router_at, router), (routes_at, routes), (segments_at, segments), (pages_at, pages)]
        )
    ]
    for copy in early:
        copy.start()
    loads = [
        pltpu.make_async_copy(query_weight, weight.at[:, 0:512], load.at[0]),
        pltpu.make_async_copy(kv_weight, weight.at[:, 512:640], load.at[1]),
        pltpu.make_async_copy(out_weight, out_w, load.at[2]),
        pltpu.make_async_copy(cache, pool, load.at[3]),
    ]
    for copy in loads:
        copy.start()

    def columns_of(phase, half):
        return pl.ds(*columns_in(phase, half))

    def remote(src, dst, send, recv, device):
        return pltpu.make_async_remote_copy(
            src_ref=src, dst_ref=dst, send_sem=send, recv_sem=recv,
            device_id={"tensor": device}, device_id_type=pl.DeviceIdType.MESH,
        )

    lane = lax.broadcasted_iota(jnp.int32, (128, 128), 1)
    sub = lax.broadcasted_iota(jnp.int32, (128, 128), 0)
    low = lane < HD // 2
    waiting = []

    def norm():
        for copy in early[:2]:
            copy.wait()
        values = hidden[...].astype(jnp.float32)
        factor = lax.rsqrt(jnp.mean(values * values, axis=-1, keepdims=True) + 1e-05)
        gains = gain[...].astype(jnp.float32)
        for c in range(D // 128):
            at = slice(c * 128, c * 128 + 128)
            full[z, x, :, at] = (values[:, at] * factor * gains[c : c + 1]).astype(jnp.bfloat16)
        pl.semaphore_wait(barrier, len(near))

    def setup(n):
        if n == 0:
            for copy in early[2:]:
                copy.wait()
        seg = segments[...]
        frequency = jnp.zeros((1, 128), jnp.float32)
        for f, value in enumerate(FREQUENCY):
            frequency = jnp.where(lax.rem(lane[0:1], HD // 2) == f, value, frequency)
        starts = [jnp.sum((seg < s).astype(jnp.float32), axis=1, keepdims=True) for s in (1, 2, 3)]
        for b in (2 * n, 2 * n + 1):
            token = (sub + b * 128).astype(jnp.float32)
            start = jnp.zeros_like(token)
            for s in starts:
                start = jnp.maximum(start, jnp.where(token >= s, s, 0.0))
            first = routes[0:1, b * 128 : b * 128 + 128].astype(jnp.float32)
            second = routes[1:2, b * 128 : b * 128 + 128].astype(jnp.float32)
            columns = jnp.where(sub == 0, first, jnp.where(sub == 1, second, 0.0)).T
            at = (b // 2, pl.ds(b % 2 * 4, 4))
            route[at] = jnp.where(lane == 2, start, columns).reshape(4, 32, 128)
            angle = (token - start) * frequency
            k = jnp.floor(angle * 0.6366197723675814 + 0.5)
            r = angle - k * 1.5703125
            r = r - k * 4.837512969970703e-4
            r = r - k * 7.549789954891882e-8
            w = r * r
            sin = r + r * w * (-1.6666654611e-1 + w * (8.3321608736e-3 - w * 1.9515295891e-4))
            cos = 1.0 - 0.5 * w + w * w * (4.166664568298827e-2 + w * (-1.388731625493765e-3 + w * 2.443315711809948e-5))
            quarter = k - 4.0 * jnp.floor(k * 0.25)
            odd = (quarter == 1.0) | (quarter == 3.0)
            c = jnp.where(odd, sin, cos)
            s = jnp.where(odd, cos, sin)
            c = jnp.where((quarter == 1.0) | (quarter == 2.0), -c, c)
            s = jnp.where(quarter >= 2.0, -s, s)
            cosine[at] = c.reshape(4, 32, 128)
            sine[at] = jnp.where(low, -s, s).reshape(4, 32, 128)
        for c in range(4 * n, 4 * n + 4):
            block = router[:, c * 128 : c * 128 + 128].astype(jnp.float32)
            block = jnp.concatenate([block, jnp.zeros((120, 128), jnp.float32)], axis=0)
            weight[c * 128 : c * 128 + 128, 640:768] = block.T.astype(jnp.bfloat16)
        if n == 0:
            kv[:, 0:2] = jnp.zeros((2, 2, NZ, ROWS, HD), jnp.bfloat16)
        if n == 3:
            for copy in loads:
                copy.wait()

    def rotate(values, c, s):
        return values * c + pltpu.roll(values, HD // 2, 1) * s

    def project(*group):
        rows = [full[fz(j)].reshape(128, D) for j in group]
        rows = rows[0] if len(group) == 1 else jnp.concatenate(rows, axis=0)
        made = jnp.dot(rows, weight[:, 512:768], preferred_element_type=jnp.float32)
        for n, j in enumerate(group):
            place_kv(j, made[n * 128 : n * 128 + 128])
        made = jnp.dot(rows, weight[:, 0:512], preferred_element_type=jnp.float32)
        for n, j in enumerate(group):
            place_queries(j, made[n * 128 : n * 128 + 128])

    def place_queries(j, made):
        za = fz(j)
        at = (slice(None), pl.ds(za, 1))
        picks = route[at].reshape(128, 128)
        c, s = cosine[at].reshape(128, 128), sine[at].reshape(128, 128)
        for n in range(2):
            local = picks[:, n : n + 1] - base.astype(jnp.float32)
            values = jnp.zeros((128, HD), jnp.float32)
            for e in range(EXPERTS):
                values = jnp.where(local == float(e), made[:, e * HD : e * HD + HD], values)
            values = rotate(values, c, s) * (HD**-0.5)
            query[(n, *at)] = values.astype(jnp.bfloat16).reshape(4, 1, 32, 128)

    def place_kv(j, made):
        za = fz(j)
        at = (slice(None), pl.ds(za, 1))
        picks = route[at].reshape(128, 128)
        c, s = cosine[at].reshape(128, 128), sine[at].reshape(128, 128)
        own = made[:, 0:128]
        own = jnp.where(parity == 0, rotate(own, c, s), own)
        kv[parity, 2:6, pl.ds(za, 1)] = own.astype(jnp.bfloat16).reshape(4, 1, 32, 128)
        rows = kv.at[parity, 2:6, za]
        copy = remote(rows, rows, kv_send.at[j], kv_recv.at[j], partner)
        copy.start()
        waiting.append(copy)
        logits = made[:, 128:256]
        lanes = lane.astype(jnp.float32)
        first = jnp.sum(jnp.where(lanes == picks[:, 0:1], logits, 0.0), axis=1, keepdims=True)
        second = jnp.sum(jnp.where(lanes == picks[:, 1:2], logits, 0.0), axis=1, keepdims=True)
        top = jnp.maximum(first, second)
        first, second = jnp.exp(first - top), jnp.exp(second - top)
        total = first + second
        gate[at] = jnp.where(lane == 0, first / total, second / total).reshape(4, 1, 32, 128)

    def swap():
        for j in Z_OFFSETS:
            zp = lax.rem(z + 1 - 2 * parity - turn * j + 2 * NZ, NZ)
            place = kv.at[1 - parity, 2:6, zp]
            remote(place, place, kv_send.at[j], kv_recv.at[j], partner).wait_recv()

    def attend(i):
        xa = fx(i)
        for half in range(2):
            at = (xa, pl.ds(half * 4, 4))
            keys = kv[0, pl.ds(xa, 3)].reshape(768, HD)[half * 128 : half * 128 + 640]
            values = kv[1, pl.ds(xa, 3)].reshape(768, HD)[half * 128 : half * 128 + 640]
            q = jnp.concatenate([query[(n, *at)].reshape(128, HD) for n in range(2)], axis=0)
            scores = lax.dot_general(q, keys, (((1,), (1,)), ((), ())), preferred_element_type=jnp.float32)
            picks = route[at].reshape(128, 128)
            gates = gate[at].reshape(128, 128)
            token = lax.broadcasted_iota(jnp.int32, (128, 640), 0) + (xa * 256 + half * 128)
            index = lax.broadcasted_iota(jnp.int32, (128, 640), 1) + ((xa - 2) * 256 + half * 128)
            allowed = (index <= token) & (index >= picks[:, 2:3].astype(jnp.int32))
            shifted = []
            for n in range(2):
                score = jnp.where(allowed, scores[n * 128 : n * 128 + 128], -1e30)
                shifted.append(jnp.exp(score - jnp.max(score, axis=1, keepdims=True)).astype(jnp.bfloat16))
            beside = jnp.concatenate([values, jnp.ones((640, HD), jnp.bfloat16)], axis=1)
            sums = jnp.dot(jnp.concatenate(shifted, axis=0), beside, preferred_element_type=jnp.float32)
            mean = sums[:, 0:HD] / sums[:, HD : 2 * HD]
            results = [mean[n * 128 : n * 128 + 128] * gates[:, n : n + 1] for n in range(2)]
            local = [picks[:, n : n + 1] - base.astype(jnp.float32) for n in range(2)]
            for e in range(EXPERTS):
                pair = jnp.where(local[0] == float(e), results[0], jnp.where(local[1] == float(e), results[1], 0.0))
                mixed[half * 128 : half * 128 + 128, e * HD : e * HD + HD] = pair.astype(jnp.bfloat16)
        for n in range(0, D, 512):
            made = jnp.dot(mixed[...], out_w[:, n : n + 512], preferred_element_type=jnp.float32)
            part[xa, :, :, n : n + 512] = made.astype(jnp.bfloat16).reshape(NZ, ROWS, 512)

    def update_cache():
        def page(p, _):
            content = pool[p].astype(jnp.float32)
            for b in range(8):
                rows = kv[parity, 2 + b // 2, pl.ds(b % 2 * 4, 4)].reshape(128, HD).astype(jnp.float32)
                hit = jnp.full((128, 128), pages[b] - p, jnp.int32) == 0
                content = jnp.where(hit, rows, content)
            pool[p] = content.astype(jnp.bfloat16)
            return 0

        lax.fori_loop(0, 16, page, 0)

    def rows_of(r):
        return pl.ds(r * PIECE, PIECE)

    def receive(half, px, pz, r, task):
        block = full.at[fz(pz), fx(px), rows_of(r), columns_of("gather", half)]
        if task["deps"]:
            at = ("AB".index(half), r, slot(px, pz))
            remote(block, block, gather_send.at[at], gather_recv.at[at], me).wait_recv()
        send(task, block, lambda n: block, gather_send, gather_recv)

    def send(task, src, dst, send_sem, recv_sem):
        for one, other, key in task["sends"]:
            _, half, px, pz, r = key
            at = ("AB".index(half), r, slot(px, pz))
            copy = remote(src, dst(at[2]), send_sem.at[at], recv_sem.at[at], device_at(one, other))
            copy.start()
            waiting.append(copy)

    def combine(half, px, pz, r, task):
        columns, rows = columns_of("reduce", half), rows_of(r)
        at = (fx(px), fz(pz), rows, columns)
        landed = landed_a if half == "A" else landed_b
        slots = [slot(*key[2:4]) for key in task["deps"]]
        for n in slots:
            place, sem = landed.at[n, rows], ("AB".index(half), r, n)
            remote(place, place, reduce_send.at[sem], reduce_recv.at[sem], me).wait_recv()
        if slots:
            total = part[at].astype(jnp.float32)
            for n in slots:
                total = total + landed[n, rows].astype(jnp.float32)
            if task["sends"]:
                part[at] = total.astype(jnp.bfloat16)
            else:
                out[rows, columns] = (total + hidden[rows, columns].astype(jnp.float32)).astype(jnp.bfloat16)
        send(task, part.at[at], lambda n: landed.at[n, rows], reduce_send, reduce_recv)

    for task in plan()[0]:
        kind, *rest = task["name"]
        if kind == "gather":
            receive(*rest, task)
        elif kind == "reduce":
            combine(*rest, task)
        elif kind == "cache":
            update_cache()
        else:
            dict(norm=norm, setup=setup, project=project, swap=swap, attend=attend)[kind](*rest)
    for copy in waiting:
        copy.wait_send()


def local(hidden, gain, router, kv_weight, query_weight, out_weight, routes, segments, pages, cache):
    vmem, hbm = pl.BlockSpec(memory_space=pltpu.VMEM), pl.BlockSpec(memory_space=pltpu.HBM)
    dma = pltpu.SemaphoreType.DMA
    return pl.pallas_call(
        layer,
        out_shape=(
            pltpu.VMEM(hidden.shape, jnp.bfloat16),
            pltpu.VMEM(cache.shape, jnp.bfloat16),
        ),
        in_specs=[hbm] * 10,
        out_specs=(vmem, vmem),
        scratch_shapes=[
            pltpu.VMEM((ROWS, D), jnp.bfloat16),
            pltpu.VMEM((D // 128, 128), jnp.bfloat16),
            pltpu.VMEM((8, D), jnp.bfloat16),
            pltpu.VMEM((2, 1024), jnp.int32),
            pltpu.VMEM((1, 1024), jnp.int32),
            pltpu.SMEM((8,), jnp.int32),
            pltpu.VMEM((NZ, NX, ROWS, D), jnp.bfloat16),
            pltpu.VMEM((NX, NZ, ROWS, D), jnp.bfloat16),
            pltpu.VMEM((SLOTS, ROWS, REDUCE_CUT), jnp.bfloat16),
            pltpu.VMEM((SLOTS, ROWS, D - REDUCE_CUT), jnp.bfloat16),
            pltpu.VMEM((D, 768), jnp.bfloat16),
            pltpu.VMEM((512, D), jnp.bfloat16),
            pltpu.VMEM((2, NX + 2, NZ, ROWS, HD), jnp.bfloat16),
            pltpu.VMEM((2, NX, NZ, ROWS, HD), jnp.bfloat16),
            pltpu.VMEM((NX, NZ, ROWS, HD), jnp.float32),
            pltpu.VMEM((NX, NZ, ROWS, HD), jnp.float32),
            pltpu.VMEM((NX, NZ, ROWS, HD), jnp.float32),
            pltpu.VMEM((NX, NZ, ROWS, HD), jnp.float32),
            pltpu.VMEM((256, 512), jnp.bfloat16),
            dma((2, PIECES, SLOTS)),
            dma((2, PIECES, SLOTS)),
            dma((2, PIECES, SLOTS)),
            dma((2, PIECES, SLOTS)),
            dma((NZ,)),
            dma((NZ,)),
            dma((10,)),
        ],
        compiler_params=pltpu.CompilerParams(
            collective_id=0, has_side_effects=True, vmem_limit_bytes=62 * 1024 * 1024
        ),
        name="layer",
    )(
        hidden, gain.reshape(D // 128, 128), router.T, kv_weight, query_weight, out_weight, routes.T,
        segments.reshape(1, -1), pages, cache,
    )


def solution(mesh):
    placed = (
        P(("dp", "tensor"), None),
        P(),
        P(),
        P(None, "tensor"),
        P(None, "tensor"),
        P("tensor", None),
        P("dp", None),
        P("dp"),
        P("dp"),
        P("dp", None, "tensor"),
    )
    return jax.shard_map(
        local,
        mesh=mesh,
        in_specs=placed,
        out_specs=(P(("dp", "tensor"), None), P("dp", None, "tensor")),
        check_vma=False,
    )
```

```python
import functools

import jax
import jax.numpy as jnp
import numpy as np
from jax import lax
from jax.experimental import pallas as pl
from jax.experimental.pallas import tpu as pltpu
from jax.sharding import PartitionSpec as P

NX, NZ, ROWS, D, HD = 4, 8, 32, 2048, 128
EXPERTS = 4
Z_OFFSETS = (0, 1, 7, 2, 6, 3, 5, 4)
GROUPS = ((0,), (1, 7), (2, 6), (3, 5), (4,))
ATTEND_ORDER = (2, 1, 3, 0)
GATHER_CUT, REDUCE_CUT = 768, 896
PIECES = 1
PIECE = ROWS // PIECES
LINK_BYTES_PER_US, LATENCY_US = 43000.0, 3.0
FREQUENCY = [float(f) for f in (10000.0 ** (-np.arange(64, dtype=np.float32) / np.float32(64))).astype(np.float32)]

RING4 = {0: (1, -1), 1: (2,)}
STAR4 = {0: (1, -1, 2)}
CHAIN8 = {0: (1, -1), 1: (2,), 2: (3,), 3: (4,), -1: (-2,), -2: (-3,)}
SKIP8 = {0: (1, 2, -1), 2: (3,), 3: (4,), -1: (-2,), -2: (-3,)}
WIDE8 = {0: (1, -1, 2, -2), 2: (3, 4), -2: (-3,)}


def turned(tree, n, sign):
    return {sign * p % n: tuple(sign * q % n for q in rest) for p, rest in tree.items()}


STAR4_TURNED = turned(STAR4, NX, 1)


def x_tree(half, pz):
    return STAR4_TURNED if half == "A" else turned(RING4, NX, 1 if pz % 2 else -1)


def z_tree(phase, half, px):
    if half == "A":
        return turned(CHAIN8, NZ, 1 if px < 2 else -1)
    return turned(SKIP8 if phase == "gather" else WIDE8, NZ, -1)


def children(phase, half, px, pz):
    found = []
    if half == "B" or pz == 0:
        found += [(q, pz) for q in x_tree(half, pz).get(px, ())]
    if half == "A" or px == 0:
        found += [(px, q) for q in z_tree(phase, half, px).get(pz, ())]
    return found


def parent(phase, half, px, pz):
    places = [(i, j) for i in range(NX) for j in range(NZ)]
    return next((p for p in places if (px, pz) in children(phase, half, *p)), None)


def links_of(one, other):
    dx, dz = (other[0] - one[0]) % NX, (other[1] - one[1]) % NZ
    if dx:
        return ("x+", 1) if dx == 1 else ("x-", 1)
    return ("z+", dz) if dz < 4 else ("z-", NZ - dz)


def move_tasks():
    tasks = []
    for half in "AB":
        for px in range(NX):
            for pz in range(NZ):
                for r in range(PIECES):
                    own = (px, pz) == (0, 0)
                    here = ("gather", half, px, pz, r)
                    sends = [((px, pz), q, ("gather", half, *q, r)) for q in children(*here[:4])]
                    tasks.append(
                        dict(name=here, deps=[] if own else [here], after=[("norm",)] if own else [], sends=sends, cost=0.06)
                    )
    for half in "AB":
        for px in ATTEND_ORDER:
            for pz in range(NZ):
                for r in range(PIECES):
                    here = ("reduce", half, px, pz, r)
                    deps = [("reduce", half, *q, r) for q in children(*here[:4])]
                    up = parent(*here[:4])
                    sends = [((px, pz), up, here)] if up else []
                    tasks.append(dict(name=here, deps=deps, after=[("attend", px)], sends=sends, cost=0.06))
    return tasks


def compute_tasks():
    tasks = [dict(name=("norm",), after=[], cost=2.0)]
    tasks += [dict(name=("setup", n), after=[], cost=0.6) for n in range(4)]
    for group in GROUPS:
        after = [("gather", half, i, j, r) for half in "AB" for i in range(NX) for j in group for r in range(PIECES)] + [("setup", n) for n in range(4)]
        tasks.append(dict(name=("project", *group), after=after, cost=0.25 + 0.75 * len(group)))
    everything = [("project", *group) for group in GROUPS]
    tasks.append(dict(name=("swap",), after=everything, cost=2.5))
    for i in ATTEND_ORDER:
        tasks.append(dict(name=("attend", i), after=[("swap",)], cost=1.75))
    tasks.append(dict(name=("cache",), after=[("swap",), ("attend", ATTEND_ORDER[-1])], cost=1.0))
    return tasks


def columns_in(phase, half):
    cut = GATHER_CUT if phase == "gather" else REDUCE_CUT
    return (0, cut) if half == "A" else (cut, D - cut)


@functools.cache
def plan():
    moves, work = move_tasks(), compute_tasks()
    clock, done, arrived, free, order = 0.0, set(), {}, {}, []
    while moves or work:
        best = None
        for task in moves:
            if all(a in done for a in task["after"]) and all(d in arrived for d in task["deps"]):
                at = max([arrived[d] for d in task["deps"]], default=0.0)
                if best is None or at < best[0]:
                    best = (at, task)
        task = None
        if best is None or best[0] > clock:
            task = next((w for w in work if all(a in done for a in w["after"])), None)
        if task is None:
            clock, task = max(clock, best[0]), best[1]
            moves.remove(task)
        else:
            work.remove(task)
        clock += task["cost"]
        for one, other, key in task.get("sends", []):
            link, hops = links_of(one, other)
            took = PIECE * columns_in(*key[:2])[1] * 2 / LINK_BYTES_PER_US
            free[link] = max(clock, free.get(link, 0.0)) + took * hops
            arrived[key] = free[link] - took * (hops - 1) + LATENCY_US
        done.add(task["name"])
        order.append(task)
    return order, clock


def slot(px, pz):
    return px * NZ + pz - 1


SLOTS = NX * NZ - 1


def layer(
    hidden_at, gain_at, router_at, kv_weight, query_weight, out_weight, routes_at, segments_at, pages_at, cache,
    out, pool,
    hidden, gain, router, routes, segments, pages,
    full, part, landed_a, landed_b, weight, out_w, kv, query, cosine, sine, route, gate, mixed,
    gather_send, gather_recv, reduce_send, reduce_recv, kv_send, kv_recv, load,
):
    me = lax.axis_index("tensor")
    turn = 1 - 2 * lax.rem(lax.axis_index("dp"), 2)
    x, z = me // NZ, lax.rem(me, NZ)
    parity = lax.rem(z, 2)
    base = parity * EXPERTS

    x_of = [lax.rem(x - turn * px + 2 * NX, NX) for px in range(NX)]
    z_of = [lax.rem(z - turn * pz + 2 * NZ, NZ) for pz in range(NZ)]
    x_steps, z_steps = [0] + [xo * NZ + z for xo in x_of[1:]], [x * NZ + zo for zo in z_of]

    def fx(px):
        return x_of[px % NX]

    def fz(pz):
        return z_of[pz % NZ]

    def device_at(one, other):
        dx, dz = (one[0] - other[0]) % NX, (one[1] - other[1]) % NZ
        return x_steps[dx] if dx else z_steps[dz]

    near = [device_at((0, 0), p) for p in ((1, 0), (-1, 0), (2, 0), (0, 1), (0, -1), (0, 2), (0, -2))]
    partner = x * NZ + z + 1 - 2 * parity

    barrier = pltpu.get_barrier_semaphore()
    for device in near:
        pl.semaphore_signal(barrier, inc=1, device_id={"tensor": device}, device_id_type=pl.DeviceIdType.MESH)

    early = [
        pltpu.make_async_copy(src, dst, load.at[4 + n])
        for n, (src, dst) in enumerate(
            [(hidden_at, hidden), (gain_at, gain), (router_at, router), (routes_at, routes), (segments_at, segments), (pages_at, pages)]
        )
    ]
    for copy in early:
        copy.start()
    loads = [
        pltpu.make_async_copy(query_weight, weight.at[:, 0:512], load.at[0]),
        pltpu.make_async_copy(kv_weight, weight.at[:, 512:640], load.at[1]),
        pltpu.make_async_copy(out_weight, out_w, load.at[2]),
        pltpu.make_async_copy(cache, pool, load.at[3]),
    ]
    for copy in loads:
        copy.start()

    def columns_of(phase, half):
        return pl.ds(*columns_in(phase, half))

    def remote(src, dst, send, recv, device):
        return pltpu.make_async_remote_copy(
            src_ref=src, dst_ref=dst, send_sem=send, recv_sem=recv,
            device_id={"tensor": device}, device_id_type=pl.DeviceIdType.MESH,
        )

    lane = lax.broadcasted_iota(jnp.int32, (128, 128), 1)
    sub = lax.broadcasted_iota(jnp.int32, (128, 128), 0)
    low = lane < HD // 2
    waiting = []

    def norm():
        for copy in early[:2]:
            copy.wait()
        values = hidden[...].astype(jnp.float32)
        factor = lax.rsqrt(jnp.mean(values * values, axis=-1, keepdims=True) + 1e-05)
        gains = gain[...].astype(jnp.float32)
        for c in range(D // 128):
            at = slice(c * 128, c * 128 + 128)
            full[z, x, :, at] = (values[:, at] * factor * gains[c : c + 1]).astype(jnp.bfloat16)
        pl.semaphore_wait(barrier, len(near))

    def setup(n):
        if n == 0:
            for copy in early[2:]:
                copy.wait()
        seg = segments[...]
        frequency = jnp.zeros((1, 128), jnp.float32)
        for f, value in enumerate(FREQUENCY):
            frequency = jnp.where(lax.rem(lane[0:1], HD // 2) == f, value, frequency)
        starts = [jnp.sum((seg < s).astype(jnp.float32), axis=1, keepdims=True) for s in (1, 2, 3)]
        for b in (2 * n, 2 * n + 1):
            token = (sub + b * 128).astype(jnp.float32)
            start = jnp.zeros_like(token)
            for s in starts:
                start = jnp.maximum(start, jnp.where(token >= s, s, 0.0))
            first = routes[0:1, b * 128 : b * 128 + 128].astype(jnp.float32)
            second = routes[1:2, b * 128 : b * 128 + 128].astype(jnp.float32)
            columns = jnp.where(sub == 0, first, jnp.where(sub == 1, second, 0.0)).T
            at = (b // 2, pl.ds(b % 2 * 4, 4))
            route[at] = jnp.where(lane == 2, start, columns).reshape(4, 32, 128)
            angle = (token - start) * frequency
            k = jnp.floor(angle * 0.6366197723675814 + 0.5)
            r = angle - k * 1.5703125
            r = r - k * 4.837512969970703e-4
            r = r - k * 7.549789954891882e-8
            w = r * r
            sin = r + r * w * (-1.6666654611e-1 + w * (8.3321608736e-3 - w * 1.9515295891e-4))
            cos = 1.0 - 0.5 * w + w * w * (4.166664568298827e-2 + w * (-1.388731625493765e-3 + w * 2.443315711809948e-5))
            quarter = k - 4.0 * jnp.floor(k * 0.25)
            odd = (quarter == 1.0) | (quarter == 3.0)
            c = jnp.where(odd, sin, cos)
            s = jnp.where(odd, cos, sin)
            c = jnp.where((quarter == 1.0) | (quarter == 2.0), -c, c)
            s = jnp.where(quarter >= 2.0, -s, s)
            cosine[at] = c.reshape(4, 32, 128)
            sine[at] = jnp.where(low, -s, s).reshape(4, 32, 128)
        for c in range(4 * n, 4 * n + 4):
            block = router[:, c * 128 : c * 128 + 128].astype(jnp.float32)
            block = jnp.concatenate([block, jnp.zeros((120, 128), jnp.float32)], axis=0)
            weight[c * 128 : c * 128 + 128, 640:768] = block.T.astype(jnp.bfloat16)
        if n == 0:
            kv[:, 0:2] = jnp.zeros((2, 2, NZ, ROWS, HD), jnp.bfloat16)
        if n == 3:
            for copy in loads:
                copy.wait()

    def rotate(values, c, s):
        return values * c + pltpu.roll(values, HD // 2, 1) * s

    def project(*group):
        rows = [full[fz(j)].reshape(128, D) for j in group]
        rows = rows[0] if len(group) == 1 else jnp.concatenate(rows, axis=0)
        made = jnp.dot(rows, weight[:, 512:768], preferred_element_type=jnp.float32)
        for n, j in enumerate(group):
            place_kv(j, made[n * 128 : n * 128 + 128])
        made = jnp.dot(rows, weight[:, 0:512], preferred_element_type=jnp.float32)
        for n, j in enumerate(group):
            place_queries(j, made[n * 128 : n * 128 + 128])

    def place_queries(j, made):
        za = fz(j)
        at = (slice(None), pl.ds(za, 1))
        picks = route[at].reshape(128, 128)
        c, s = cosine[at].reshape(128, 128), sine[at].reshape(128, 128)
        for n in range(2):
            local = picks[:, n : n + 1] - base.astype(jnp.float32)
            values = jnp.zeros((128, HD), jnp.float32)
            for e in range(EXPERTS):
                values = jnp.where(local == float(e), made[:, e * HD : e * HD + HD], values)
            values = rotate(values, c, s) * (HD**-0.5)
            query[(n, *at)] = values.astype(jnp.bfloat16).reshape(4, 1, 32, 128)

    def place_kv(j, made):
        za = fz(j)
        at = (slice(None), pl.ds(za, 1))
        picks = route[at].reshape(128, 128)
        c, s = cosine[at].reshape(128, 128), sine[at].reshape(128, 128)
        own = made[:, 0:128]
        own = jnp.where(parity == 0, rotate(own, c, s), own)
        kv[parity, 2:6, pl.ds(za, 1)] = own.astype(jnp.bfloat16).reshape(4, 1, 32, 128)
        rows = kv.at[parity, 2:6, za]
        copy = remote(rows, rows, kv_send.at[j], kv_recv.at[j], partner)
        copy.start()
        waiting.append(copy)
        logits = made[:, 128:256]
        lanes = lane.astype(jnp.float32)
        first = jnp.sum(jnp.where(lanes == picks[:, 0:1], logits, 0.0), axis=1, keepdims=True)
        second = jnp.sum(jnp.where(lanes == picks[:, 1:2], logits, 0.0), axis=1, keepdims=True)
        top = jnp.maximum(first, second)
        first, second = jnp.exp(first - top), jnp.exp(second - top)
        total = first + second
        gate[at] = jnp.where(lane == 0, first / total, second / total).reshape(4, 1, 32, 128)

    def swap():
        for j in Z_OFFSETS:
            zp = lax.rem(z + 1 - 2 * parity - turn * j + 2 * NZ, NZ)
            place = kv.at[1 - parity, 2:6, zp]
            remote(place, place, kv_send.at[j], kv_recv.at[j], partner).wait_recv()

    def attend(i):
        xa = fx(i)
        for half in range(2):
            at = (xa, pl.ds(half * 4, 4))
            keys = kv[0, pl.ds(xa, 3)].reshape(768, HD)[half * 128 : half * 128 + 640]
            values = kv[1, pl.ds(xa, 3)].reshape(768, HD)[half * 128 : half * 128 + 640]
            q = jnp.concatenate([query[(n, *at)].reshape(128, HD) for n in range(2)], axis=0)
            scores = lax.dot_general(q, keys, (((1,), (1,)), ((), ())), preferred_element_type=jnp.float32)
            picks = route[at].reshape(128, 128)
            gates = gate[at].reshape(128, 128)
            token = lax.broadcasted_iota(jnp.int32, (128, 640), 0) + (xa * 256 + half * 128)
            index = lax.broadcasted_iota(jnp.int32, (128, 640), 1) + ((xa - 2) * 256 + half * 128)
            allowed = (index <= token) & (index >= picks[:, 2:3].astype(jnp.int32))
            shifted = []
            for n in range(2):
                score = jnp.where(allowed, scores[n * 128 : n * 128 + 128], -1e30)
                shifted.append(jnp.exp(score - jnp.max(score, axis=1, keepdims=True)).astype(jnp.bfloat16))
            beside = jnp.concatenate([values, jnp.ones((640, HD), jnp.bfloat16)], axis=1)
            sums = jnp.dot(jnp.concatenate(shifted, axis=0), beside, preferred_element_type=jnp.float32)
            mean = sums[:, 0:HD] / sums[:, HD : 2 * HD]
            results = [mean[n * 128 : n * 128 + 128] * gates[:, n : n + 1] for n in range(2)]
            local = [picks[:, n : n + 1] - base.astype(jnp.float32) for n in range(2)]
            for e in range(EXPERTS):
                pair = jnp.where(local[0] == float(e), results[0], jnp.where(local[1] == float(e), results[1], 0.0))
                mixed[half * 128 : half * 128 + 128, e * HD : e * HD + HD] = pair.astype(jnp.bfloat16)
        for n in range(0, D, 512):
            made = jnp.dot(mixed[...], out_w[:, n : n + 512], preferred_element_type=jnp.float32)
            part[xa, :, :, n : n + 512] = made.astype(jnp.bfloat16).reshape(NZ, ROWS, 512)

    def update_cache():
        def page(p, _):
            content = pool[p].astype(jnp.float32)
            for b in range(8):
                rows = kv[parity, 2 + b // 2, pl.ds(b % 2 * 4, 4)].reshape(128, HD).astype(jnp.float32)
                hit = jnp.full((128, 128), pages[b] - p, jnp.int32) == 0
                content = jnp.where(hit, rows, content)
            pool[p] = content.astype(jnp.bfloat16)
            return 0

        lax.fori_loop(0, 16, page, 0)

    def rows_of(r):
        return pl.ds(r * PIECE, PIECE)

    def receive(half, px, pz, r, task):
        block = full.at[fz(pz), fx(px), rows_of(r), columns_of("gather", half)]
        if task["deps"]:
            at = ("AB".index(half), r, slot(px, pz))
            remote(block, block, gather_send.at[at], gather_recv.at[at], me).wait_recv()
        send(task, block, lambda n: block, gather_send, gather_recv)

    def send(task, src, dst, send_sem, recv_sem):
        for one, other, key in task["sends"]:
            _, half, px, pz, r = key
            at = ("AB".index(half), r, slot(px, pz))
            copy = remote(src, dst(at[2]), send_sem.at[at], recv_sem.at[at], device_at(one, other))
            copy.start()
            waiting.append(copy)

    def combine(half, px, pz, r, task):
        columns, rows = columns_of("reduce", half), rows_of(r)
        at = (fx(px), fz(pz), rows, columns)
        landed = landed_a if half == "A" else landed_b
        slots = [slot(*key[2:4]) for key in task["deps"]]
        for n in slots:
            place, sem = landed.at[n, rows], ("AB".index(half), r, n)
            remote(place, place, reduce_send.at[sem], reduce_recv.at[sem], me).wait_recv()
        if slots:
            total = part[at].astype(jnp.float32)
            for n in slots:
                total = total + landed[n, rows].astype(jnp.float32)
            if task["sends"]:
                part[at] = total.astype(jnp.bfloat16)
            else:
                out[rows, columns] = (total + hidden[rows, columns].astype(jnp.float32)).astype(jnp.bfloat16)
        send(task, part.at[at], lambda n: landed.at[n, rows], reduce_send, reduce_recv)

    for task in plan()[0]:
        kind, *rest = task["name"]
        if kind == "gather":
            receive(*rest, task)
        elif kind == "reduce":
            combine(*rest, task)
        elif kind == "cache":
            update_cache()
        else:
            dict(norm=norm, setup=setup, project=project, swap=swap, attend=attend)[kind](*rest)
    for copy in waiting:
        copy.wait_send()


def local(hidden, gain, router, kv_weight, query_weight, out_weight, routes, segments, pages, cache):
    vmem, hbm = pl.BlockSpec(memory_space=pltpu.VMEM), pl.BlockSpec(memory_space=pltpu.HBM)
    dma = pltpu.SemaphoreType.DMA
    return pl.pallas_call(
        layer,
        out_shape=(
            pltpu.VMEM(hidden.shape, jnp.bfloat16),
            pltpu.VMEM(cache.shape, jnp.bfloat16),
        ),
        in_specs=[hbm] * 10,
        out_specs=(vmem, vmem),
        scratch_shapes=[
            pltpu.VMEM((ROWS, D), jnp.bfloat16),
            pltpu.VMEM((D // 128, 128), jnp.bfloat16),
            pltpu.VMEM((8, D), jnp.bfloat16),
            pltpu.VMEM((2, 1024), jnp.int32),
            pltpu.VMEM((1, 1024), jnp.int32),
            pltpu.SMEM((8,), jnp.int32),
            pltpu.VMEM((NZ, NX, ROWS, D), jnp.bfloat16),
            pltpu.VMEM((NX, NZ, ROWS, D), jnp.bfloat16),
            pltpu.VMEM((SLOTS, ROWS, REDUCE_CUT), jnp.bfloat16),
            pltpu.VMEM((SLOTS, ROWS, D - REDUCE_CUT), jnp.bfloat16),
            pltpu.VMEM((D, 768), jnp.bfloat16),
            pltpu.VMEM((512, D), jnp.bfloat16),
            pltpu.VMEM((2, NX + 2, NZ, ROWS, HD), jnp.bfloat16),
            pltpu.VMEM((2, NX, NZ, ROWS, HD), jnp.bfloat16),
            pltpu.VMEM((NX, NZ, ROWS, HD), jnp.float32),
            pltpu.VMEM((NX, NZ, ROWS, HD), jnp.float32),
            pltpu.VMEM((NX, NZ, ROWS, HD), jnp.float32),
            pltpu.VMEM((NX, NZ, ROWS, HD), jnp.float32),
            pltpu.VMEM((256, 512), jnp.bfloat16),
            dma((2, PIECES, SLOTS)),
            dma((2, PIECES, SLOTS)),
            dma((2, PIECES, SLOTS)),
            dma((2, PIECES, SLOTS)),
            dma((NZ,)),
            dma((NZ,)),
            dma((10,)),
        ],
        compiler_params=pltpu.CompilerParams(
            collective_id=0, has_side_effects=True, vmem_limit_bytes=62 * 1024 * 1024
        ),
        name="layer",
    )(
        hidden, gain.reshape(D // 128, 128), router.T, kv_weight, query_weight, out_weight, routes.T,
        segments.reshape(1, -1), pages, cache,
    )


def solution(mesh):
    placed = (
        P(("dp", "tensor"), None),
        P(),
        P(),
        P(None, "tensor"),
        P(None, "tensor"),
        P("tensor", None),
        P("dp", None),
        P("dp"),
        P("dp"),
        P("dp", None, "tensor"),
    )
    return jax.shard_map(
        local,
        mesh=mesh,
        in_specs=placed,
        out_specs=(P(("dp", "tensor"), None), P("dp", None, "tensor")),
        check_vma=False,
    )
```
